32 devices in a mesh: pos: 8 (over y, x, core), freq: 4 (over z).
Axes of the slice: x: 2, y: 2, z: 4, core: 2. Of those that a mesh axis runs over, the one named last changes fastest.
Arguments:
- footprint: int32 [16, 32], replicated, may hold values from 0 to 255, as said below
- basis: bfloat16 [16, 16, 2048, 256], P('pos', 'freq'), may hold values from -0.125 to 0.125
- weights: float32 [256], replicated, may hold values from 0.1 to 10
- conduct: float32 [2, 32, 256], P(None, 'pos', 'freq'), may hold values from 0.08 to 0.24
- baseline: float32 [32, 256], P('pos', 'freq'), may hold values from 0.2 to 2
Outputs:
- image: float32 [32, 256], P('pos', 'freq')
The draws below stay inside these ranges and needn't reach their ends.
Inputs may be any that keep to these rules, and one draw needn't show every extreme that they name: `footprint`: tile t belongs to owner t // 32. Among the 64 entries of the rows of one index of pos, at most 16 lie in one owner's tiles, and in every draw one owner gets exactly 16 from every index of pos. Entries may repeat.
All inputs are finite; a program needn't handle non-finite values.
Results may differ from the reference program's by a relative error of at most 0.0003.
Values sent between devices are 32-bit elements; how exact they have to be, the bound alone decides.
No kernel may reach another device: no remote copies, remote signals or barrier semaphores. Data moves between devices by JAX's collectives and lax.ppermute only.
A program may use at most 64 MiB of HBM per device.

```python
import math
import jax
import jax.numpy as jnp
from jax import lax

ELEM = 1024
R = 256
FREQS = 16
POS_DEV = 2
FOOT = 32
TH = 4
TW = 8
TILE_DEV = 32
PASSES = 3
POSITIONS = 16
TILES = 256
CAP = 16
NX = 32
NZ = 256
N_POS = 8


def draw_footprint(key, part):
    owner_count = TILES // TILE_DEV
    block_rows = POS_DEV * FOOT
    slot_count = owner_count * CAP
    hot_owner = jax.random.randint(jax.random.fold_in(key, 1), (), 0, owner_count)

    def one_block(block_key):
        slot_ids = jnp.arange(slot_count)
        slot_owner = slot_ids // CAP
        shuffled = jax.random.permutation(jax.random.fold_in(block_key, 2), slot_count)
        forced = (slot_ids == 0) | (slot_ids == slot_count - CAP)
        score = jnp.where(slot_owner == hot_owner, slot_ids - 2 * slot_count, jnp.where(forced, slot_ids - slot_count, shuffled))
        picked = slot_owner[jnp.argsort(score)[:block_rows]]
        within = jax.random.randint(jax.random.fold_in(block_key, 3), (block_rows,), 0, TILE_DEV)
        within = within.at[jnp.argmax(picked == owner_count - 1)].set(TILE_DEV - 1)
        within = within.at[jnp.argmax(picked == 0)].set(0)
        mixing = jax.random.permutation(jax.random.fold_in(block_key, 4), block_rows)
        return (picked * TILE_DEV + within)[mixing]
    block_keys = jax.vmap(lambda index: jax.random.fold_in(key, index + 10))(jnp.arange(POSITIONS // POS_DEV))
    return jax.vmap(one_block)(block_keys).reshape(POSITIONS, FOOT).astype(jnp.int32)


def steps_of(own_key, dims, cuts, smallest, high):
    gain = 1.0
    for dim, parts in cuts:
        heights = jax.random.uniform(jax.random.fold_in(jax.random.fold_in(own_key, 6), dim), (parts,), jnp.float32, smallest / len(cuts), high / len(cuts))
        gain = gain * jnp.repeat(jnp.exp(heights), dims[dim] // parts).reshape((-1,) + (1,) * (len(dims) - 1 - dim))
    return gain


def noise(rng, dims, spread, limit, split=(), held_as=jnp.bfloat16):
    level = steps_of(rng, dims, split, -0.22, 0.18) if split else 1.0
    array = jax.random.normal(rng, dims, jnp.float32) * spread * level
    return jnp.minimum(jnp.maximum(array, -limit), limit).astype(held_as)


def setup_inputs(seed: int = 0) -> dict:
    keys = jax.random.split(jax.random.key(seed), 6)
    return {
        "footprint": draw_footprint(jax.random.fold_in(keys[5], 71), 0),
        "basis": noise(keys[1], (POSITIONS, FREQS, 2 * ELEM, R), (2 * ELEM) ** -0.5, 0.125, ((0, 8), (1, 4))),
        "weights": jnp.clip(jnp.exp(jax.random.uniform(keys[2], (R,), jnp.float32, math.log(0.1), math.log(10.0))), 0.1, 10.0),
        "conduct": jnp.clip(0.08 + 0.16 * jax.random.uniform(keys[3], (2, NX, NZ), jnp.float32) ** steps_of(keys[3], (2, NX, NZ), ((1, 8), (2, 4)), -0.2, 0.2), 0.08, 0.24),
        "baseline": jnp.clip(0.2 + 1.8 * jax.random.uniform(keys[4], (NX, NZ), jnp.float32) ** steps_of(keys[4], (NX, NZ), ((0, 8), (1, 4)), -0.2, 0.2), 0.2, 2.0),
    }


elem_pitch = 0.125
cell_spacing = 0.7
top_depth = 4.0
eps_value = 1e-06

def green_rows(tile_ids, pos_global, freq_global, elements, positions, freqs):
    cells = jnp.arange(TH * TW)
    grid_row = (tile_ids // TILE_DEV)[:, None] * TH + (cells // TW)[None, :]
    grid_col = (tile_ids % TILE_DEV)[:, None] * TW + (cells % TW)[None, :]
    depth = top_depth + cell_spacing * grid_row.reshape(-1).astype(jnp.float32)
    lateral = cell_spacing * grid_col.reshape(-1).astype(jnp.float32)
    centre = pos_global.astype(jnp.float32) * (cell_spacing * TW * TILE_DEV / positions)
    element = (jnp.arange(elements).astype(jnp.float32) - 0.5 * (elements - 1)) * elem_pitch + centre
    across = lateral[:, None] - element[None, :]
    distance = jnp.sqrt(depth[:, None] * depth[:, None] + across * across)
    wavenum = 2.0 * math.pi * (0.5 + freq_global.astype(jnp.float32) / freqs)
    amplitude = jnp.sqrt(top_depth / distance)
    phase = wavenum * distance
    return jnp.concatenate([amplitude * jnp.cos(phase), amplitude * jnp.sin(phase)], axis=1).astype(jnp.bfloat16)

def relax(values, across_k, along_k):
    centre_x = across_k[1:-1, 1:-1]
    centre_z = along_k[1:-1, 1:-1]
    middle = values[1:-1, 1:-1]
    north = jnp.minimum(centre_x, across_k[:-2, 1:-1]) * (values[:-2, 1:-1] - middle)
    south = jnp.minimum(centre_x, across_k[2:, 1:-1]) * (values[2:, 1:-1] - middle)
    west = jnp.minimum(centre_z, along_k[1:-1, :-2]) * (values[1:-1, :-2] - middle)
    east = jnp.minimum(centre_z, along_k[1:-1, 2:]) * (values[1:-1, 2:] - middle)
    return middle + north + south + west + east

def reference(footprint, basis, weights, conduct, baseline):
    tile_cells = TH * TW

    def one_position(pos_index):
        tile_ids = footprint[pos_index]

        def add_freq(running, freq_index):
            green = green_rows(tile_ids, pos_index, freq_index, ELEM, POSITIONS, FREQS)
            return (running + jnp.dot(green, basis[pos_index, freq_index], preferred_element_type=jnp.float32), None)
        start = jnp.zeros((FOOT * tile_cells, R), jnp.float32)
        total, _ = lax.scan(add_freq, start, jnp.arange(FREQS))
        return total
    coeffs = lax.map(one_position, jnp.arange(POSITIONS))
    compound = jnp.zeros((TILES, tile_cells, R), jnp.float32).at[footprint.reshape(-1)].add(coeffs.reshape(POSITIONS * FOOT, tile_cells, R))
    intensity = jnp.sqrt(lax.optimization_barrier(jnp.sum(compound * compound * weights, axis=-1)) / R + eps_value)
    grid = intensity.reshape(N_POS, TILE_DEV, TH, TW).transpose(0, 2, 1, 3).reshape(N_POS * TH, TILE_DEV * TW)
    grid = grid + baseline
    across_k = jnp.pad(conduct[0], 1)
    along_k = jnp.pad(conduct[1], 1)
    for sweep in range(PASSES):
        grid = relax(jnp.pad(grid, 1), across_k, along_k)
    return grid
```

```python
import functools

import jax
import jax.numpy as jnp
from jax import lax
from jax.experimental import pallas as pl
from jax.experimental.pallas import tpu as pltpu
from jax.sharding import PartitionSpec as P

TH = 4
TW = 8
CELLS = TH * TW
TILE_DEV = 32
PASSES = 3
LANES = 128
ELEM_BLOCK = 256

elem_pitch = 0.125
cell_spacing = 0.7
top_depth = 4.0
eps_value = 1e-06

COS_PI = (0.9999999403953552, -4.934792995452881, 4.058411121368408, -1.331876516342163, 0.21968960762023926)
SIN_PI = (3.1415927410125732, -5.167710304260254, 2.550077438354492, -0.598291277885437, 0.07765766233205795)

HIGHEST = lax.Precision.HIGHEST
VMEM_LIMIT = 48 * 1024 * 1024


def half_turn(turns):
    x = turns - jnp.round(turns)
    square = x * x
    c = COS_PI[-1]
    for term in COS_PI[-2::-1]:
        c = c * square + term
    s = SIN_PI[-1]
    for term in SIN_PI[-2::-1]:
        s = s * square + term
    return c, s * x


def waves(distance, inverse, centre_turns, half_step, count):
    c, s = half_turn(centre_turns * distance)
    amplitude = 2.0 * (inverse * lax.rsqrt(inverse))
    twice = (amplitude + amplitude) * c
    mid_c = twice * c - amplitude
    mid_s = twice * s
    c, s = half_turn(half_step * distance)
    twice = c + c
    step_c = twice * c - 1.0
    step_s = twice * s
    cc, ss, cs, sc = mid_c * step_c, mid_s * step_s, mid_c * step_s, mid_s * step_c
    low, high = (cc + ss, sc - cs), (cc - ss, sc + cs)
    lows, highs = [low], [high]
    factor = 4.0 * (step_c * step_c) - 2.0
    before_low, before_high = high, low
    for _ in range(count // 2 - 1):
        low, before_low = tuple(factor * a - b for a, b in zip(low, before_low)), low
        high, before_high = tuple(factor * a - b for a, b in zip(high, before_high)), high
        lows.append(low)
        highs.append(high)
    return lows[::-1] + highs


def project_kernel(sizes, part, where_ref, foot_ref, basis_ref, *refs):
    pos_count, freqs, positions, elements, pos_local, freq_local, foot = sizes
    groups = pos_count // TH
    per_dest = TW // groups
    out_refs, (green_ref, total_ref) = refs[:groups], refs[groups:]
    offset, block = pl.program_id(0), pl.program_id(1)
    my_pos, my_freq = where_ref[0], where_ref[1]
    pos_global = my_pos * pos_local + offset
    cell_row = (my_pos // groups) ^ part
    my_group = lax.rem(my_pos, groups)
    first_freq = (my_freq * freq_local).astype(jnp.float32)
    centre_turns = 0.5 + (first_freq + 0.5 * (freq_local - 1)) / freqs
    half_step = 0.5 / freqs
    centre = pos_global.astype(jnp.float32) * (cell_spacing * TW * TILE_DEV / positions)

    row = lax.broadcasted_iota(jnp.int32, (16, LANES), 0)
    sub = row % TW
    cell_col = ((sub // per_dest) ^ my_group) * per_dest + sub % per_dest
    lane = lax.broadcasted_iota(jnp.int32, (16, LANES), 1)

    def rows(pair, _):
        first = foot_ref[pos_global, 2 * pair]
        second = foot_ref[pos_global, 2 * pair + 1]
        tile = jnp.where(row < TW, first, second)
        tile_row, tile_col = tile // TILE_DEV, tile % TILE_DEV
        grid_row = (tile_row * TH + cell_row).astype(jnp.float32)
        grid_col = (tile_col * TW + cell_col).astype(jnp.float32)
        depth = top_depth + cell_spacing * grid_row
        depth_square = depth * depth
        lateral = cell_spacing * grid_col
        for piece in range(ELEM_BLOCK // LANES):
            index = (block * ELEM_BLOCK + piece * LANES + lane).astype(jnp.float32)
            element = (index - 0.5 * (elements - 1)) * elem_pitch + centre
            across = lateral - element
            square = depth_square + across * across
            inverse = lax.rsqrt(square)
            distance = square * inverse
            for number, pair_of in enumerate(waves(distance, inverse, centre_turns, half_step, freq_local)):
                for part_of, wave in enumerate(pair_of):
                    start = (number * 2 + part_of) * ELEM_BLOCK + piece * LANES
                    green_ref[pl.ds(pl.multiple_of(pair * 16, 16), 16), start : start + LANES] = wave.astype(
                        jnp.bfloat16
                    )
        return 0

    lax.fori_loop(0, foot // 2, rows, 0)
    gain = jnp.dot(
        green_ref[...],
        basis_ref[...].reshape(freq_local * 2 * ELEM_BLOCK, -1),
        preferred_element_type=jnp.float32,
    )

    spans = [slice(start, start + LANES) for start in range(0, gain.shape[1], LANES)]

    @pl.when(block == 0)
    def _():
        for half, span in enumerate(spans):
            total_ref[half] = gain[:, span]

    @pl.when(block > 0)
    def _():
        for half, span in enumerate(spans):
            total_ref[half] = total_ref[half] + gain[:, span]

    @pl.when(block == pl.num_programs(1) - 1)
    def _():
        for group in range(groups):
            for cell in range(per_dest):
                for half, span in enumerate(spans):
                    out_refs[group][cell, :, span] = total_ref[half, pl.ds(group * per_dest + cell, foot, stride=TW), :]


def project(sizes, part, where, footprint, basis):
    pos_count, freqs, positions, elements, pos_local, freq_local, foot = sizes
    groups = pos_count // TH
    per_dest = TW // groups
    rank = basis.shape[-1]
    blocks = elements // ELEM_BLOCK
    rows = foot * TW
    flops = 2 * pos_local * rows * freq_local * 2 * elements * rank
    return pl.pallas_call(
        functools.partial(project_kernel, sizes, part),
        grid=(pos_local, blocks),
        in_specs=[
            pl.BlockSpec(memory_space=pltpu.SMEM),
            pl.BlockSpec(memory_space=pltpu.SMEM),
            pl.BlockSpec((None, freq_local, 2, ELEM_BLOCK, rank), lambda p, e: (p, 0, 0, e, 0)),
        ],
        out_specs=[pl.BlockSpec((per_dest, foot, rank), lambda p, e: (0, p, 0))] * groups,
        out_shape=[jax.ShapeDtypeStruct((per_dest, pos_local * foot, rank), jnp.float32)] * groups,
        scratch_shapes=[
            pltpu.VMEM((rows, freq_local * 2 * ELEM_BLOCK), jnp.bfloat16),
            pltpu.VMEM((rank // LANES, rows, LANES), jnp.float32),
        ],
        compiler_params=pltpu.CompilerParams(vmem_limit_bytes=VMEM_LIMIT),
        cost_estimate=pl.CostEstimate(flops=flops, bytes_accessed=basis.size * 2, transcendentals=0),
        name=f"project_{part}",
    )(where, footprint, basis)


def three_terms(values):
    high = values.astype(jnp.bfloat16)
    rest = values - high.astype(jnp.float32)
    mid = rest.astype(jnp.bfloat16)
    return high, mid, (rest - mid.astype(jnp.float32)).astype(jnp.bfloat16)


def gather_kernel(pos_count, freq_count, tile_rows, where_ref, ids_ref, *refs):
    in_refs, out_refs = refs[:pos_count], refs[pos_count:]
    cells, entries, rank = in_refs[0].shape
    shard = out_refs[0].shape[1]
    tile_cols = shard // tile_rows
    groups = pos_count // TH
    my_pos, my_freq = where_ref[0], where_ref[1]
    left = (lax.rem(my_pos, groups) * 2 >= groups).astype(jnp.int32)
    row = lax.broadcasted_iota(jnp.int32, (shard, entries), 0)
    wanted = (row % tile_rows) * TILE_DEV + row // tile_rows - left
    hot = []
    for other in range(freq_count):
        base = (my_freq ^ other) * (tile_cols - 1)
        col = row // tile_rows - left + base
        hot_row = []
        for source in range(pos_count):
            ids = ids_ref[pl.ds(my_pos ^ source, 1), :]
            hit = (wanted + base == ids) & (col >= 0) & (col < TILE_DEV)
            hot_row.append(hit.astype(jnp.float32).astype(jnp.bfloat16))
        hot_row = jnp.concatenate(hot_row, axis=1)
        hot.append(jnp.concatenate([hot_row] * 3, axis=1))
    for cell in range(cells):
        values = jnp.concatenate([ref[cell] for ref in in_refs], axis=0)
        terms = jnp.concatenate(three_terms(values), axis=0)
        for other in range(freq_count):
            out_refs[other][cell] = jnp.dot(hot[other], terms, preferred_element_type=jnp.float32)


def gather_tiles(freq_count, where, ids, parts):
    pos_count = len(parts)
    cells, entries, rank = parts[0].shape
    tile_rows = pos_count
    shard = (TILE_DEV // freq_count + 1) * tile_rows
    return pl.pallas_call(
        functools.partial(gather_kernel, pos_count, freq_count, tile_rows),
        in_specs=[pl.BlockSpec(memory_space=pltpu.SMEM)] + [pl.BlockSpec(memory_space=pltpu.VMEM)] * (1 + pos_count),
        out_specs=[pl.BlockSpec(memory_space=pltpu.VMEM)] * freq_count,
        out_shape=[jax.ShapeDtypeStruct((cells, shard, rank), jnp.float32)] * freq_count,
        compiler_params=pltpu.CompilerParams(vmem_limit_bytes=VMEM_LIMIT),
        name="tiles",
    )(where, ids, *parts)


def energy_kernel(freq_count, weights_ref, rims_ref, left_ref, right_ref, *refs):
    in_refs, out_ref = refs[:freq_count], refs[freq_count]
    cells, shard, rank = in_refs[0].shape
    weights = jnp.broadcast_to(weights_ref[...], (8, rank))
    for cell in range(cells):
        summed = in_refs[0][cell]
        for ref in in_refs[1:]:
            summed = summed + ref[cell]
        energy = lax.dot_general(
            weights,
            summed * summed,
            (((1,), (1,)), ((), ())),
            precision=HIGHEST,
            preferred_element_type=jnp.float32,
        )
        out_ref[pl.ds(cell, 1), 0:shard] = jnp.sqrt(energy[0:1] / rank + eps_value)
    rims, edge = rims_ref.shape, left_ref.shape[1]
    out_ref[cells : cells + rims[0], 0 : rims[1]] = rims_ref[...]
    out_ref[cells : cells + rims[0], rims[1] : rims[1] + edge] = right_ref[...]
    out_ref[cells : cells + rims[0], out_ref.shape[1] - edge :] = left_ref[...]


def energies(weights, rims, left, right, shards):
    cells, shard, rank = shards[0].shape
    rows = cells + rims.shape[0]
    width = -(-max(shard, rims.shape[1] + 2 * left.shape[1]) // LANES) * LANES
    return pl.pallas_call(
        functools.partial(energy_kernel, len(shards)),
        in_specs=[pl.BlockSpec(memory_space=pltpu.VMEM)] * (4 + len(shards)),
        out_specs=pl.BlockSpec(memory_space=pltpu.VMEM),
        out_shape=jax.ShapeDtypeStruct((rows, width), jnp.float32),
        compiler_params=pltpu.CompilerParams(vmem_limit_bytes=VMEM_LIMIT),
        name="energies",
    )(weights, rims, left, right, *shards)


def diffuse_kernel(cells, shard, where_ref, strips_ref, out_ref, field_ref):
    pos_count, _, width = strips_ref.shape
    tile_rows = pos_count
    tile_cols = shard // tile_rows
    groups = pos_count // TH
    my_pos = where_ref[0]
    tile_row = lax.broadcasted_iota(jnp.int32, (tile_rows, width), 0)
    spot = lax.broadcasted_iota(jnp.int32, (tile_rows, width), 1)
    here = (spot % tile_rows == tile_row) & (spot < shard)
    source = lax.broadcasted_iota(jnp.int32, (width, LANES), 0)
    target = lax.broadcasted_iota(jnp.int32, (width, LANES), 1)
    field = [jnp.zeros((tile_rows, LANES), jnp.float32) for _ in range(TH)]
    for group in range(groups):
        left = 1 if group * 2 >= groups else 0
        for cell in range(cells):
            col = (source // tile_rows - left) * TW + group * cells + cell
            place = ((target == (col + LANES) % LANES) & (source < shard)).astype(jnp.float32)
            for row in range(TH):
                line = strips_ref[row * groups + group, pl.ds(cell, 1), :]
                spread = jnp.where(here, jnp.broadcast_to(line, (tile_rows, width)), 0.0)
                field[row] = field[row] + jnp.dot(
                    spread, place, precision=HIGHEST, preferred_element_type=jnp.float32
                )

    def strip(which, row):
        return strips_ref[:, cells + which * TH + row, 0:LANES]

    across_k = [strip(0, row) for row in range(TH)]
    along_k = [strip(1, row) for row in range(TH)]
    field = [field[row] + strip(2, row) for row in range(TH)]

    def above(rows, row):
        if row:
            return rows[row - 1]
        return jnp.where(tile_row[:, :LANES] == 0, 0.0, pltpu.roll(rows[TH - 1], 1, 0))

    def below(rows, row):
        if row < TH - 1:
            return rows[row + 1]
        return jnp.where(tile_row[:, :LANES] == tile_rows - 1, 0.0, pltpu.roll(rows[0], tile_rows - 1, 0))

    north_k = [jnp.minimum(across_k[r], above(across_k, r)) for r in range(TH)]
    south_k = [jnp.minimum(across_k[r], below(across_k, r)) for r in range(TH)]
    west_k = [jnp.minimum(k, pltpu.roll(k, 1, 1)) for k in along_k]
    east_k = [jnp.minimum(k, pltpu.roll(k, LANES - 1, 1)) for k in along_k]
    for _ in range(PASSES):
        field = [
            field[r]
            + north_k[r] * (above(field, r) - field[r])
            + south_k[r] * (below(field, r) - field[r])
            + west_k[r] * (pltpu.roll(field[r], 1, 1) - field[r])
            + east_k[r] * (pltpu.roll(field[r], LANES - 1, 1) - field[r])
            for r in range(TH)
        ]
    for row in range(TH):
        field_ref[...] = field[row]
        out_ref[pl.ds(row, 1), :] = field_ref[pl.ds(my_pos, 1), 0 : out_ref.shape[1]]


def diffuse(cells, shard, where, strips, columns):
    return pl.pallas_call(
        functools.partial(diffuse_kernel, cells, shard),
        in_specs=[pl.BlockSpec(memory_space=pltpu.SMEM), pl.BlockSpec(memory_space=pltpu.VMEM)],
        out_specs=pl.BlockSpec(memory_space=pltpu.VMEM),
        out_shape=jax.ShapeDtypeStruct((TH, columns), jnp.float32),
        scratch_shapes=[pltpu.VMEM((strips.shape[0], LANES), jnp.float32)],
        compiler_params=pltpu.CompilerParams(vmem_limit_bytes=VMEM_LIMIT),
        name="diffuse",
    )(where, strips)


def swap(array, axis, distance):
    return lax.ppermute(array, axis, [(i, i ^ distance) for i in range(lax.axis_size(axis))])


def body(footprint, basis, weights, conduct, baseline):
    pos_local, freq_local, doubled, rank = basis.shape
    elements = doubled // 2
    foot = footprint.shape[1]
    pos_count = lax.axis_size("pos")
    freq_count = lax.axis_size("freq")
    columns = baseline.shape[1]
    sizes = (
        pos_count,
        freq_local * freq_count,
        pos_local * pos_count,
        elements,
        pos_local,
        freq_local,
        foot,
    )
    where = jnp.stack([lax.axis_index("pos"), lax.axis_index("freq")]).astype(jnp.int32)
    ids = footprint.reshape(pos_count, pos_local * foot)
    rims = jnp.concatenate([conduct[0], conduct[1], baseline], axis=0)
    left = lax.ppermute(rims[:, columns - TW :], "freq", [(i, i + 1) for i in range(freq_count - 1)])
    right = lax.ppermute(rims[:, :TW], "freq", [(i + 1, i) for i in range(freq_count - 1)])
    split = basis.reshape(pos_local, freq_local, 2, elements, rank)
    groups = pos_count // TH
    parts = [None] * pos_count
    for part in range(TH - 1, -1, -1):
        sent = project(sizes, part, where, footprint, split)
        for group in range(groups):
            distance = part * groups + group
            parts[distance] = swap(sent[group], "pos", distance) if distance else sent[group]
    tiles = gather_tiles(freq_count, where, ids, parts)
    shards = [swap(tiles[d], "freq", d) if d else tiles[d] for d in range(freq_count)]
    strip = energies(weights.reshape(1, rank), rims, left, right, shards)
    strips = lax.all_gather(strip, "pos")
    return diffuse(CELLS // pos_count, shards[0].shape[1], where, strips, columns)


def solution(mesh):
    return jax.shard_map(
        body,
        mesh=mesh,
        in_specs=(P(), P("pos", "freq", None, None), P(), P(None, "pos", "freq"), P("pos", "freq")),
        out_specs=P("pos", "freq"),
        check_vma=False,
    )
```

```python
import functools
import math

import jax
import jax.numpy as jnp
from jax import lax
from jax.experimental import pallas as pl
from jax.experimental.pallas import tpu as pltpu
from jax.sharding import PartitionSpec as P

TH = 4
TW = 8
CELLS = TH * TW
TILE_DEV = 32
PASSES = 3
LANES = 128
ELEM_BLOCK = 256

elem_pitch = 0.125
cell_spacing = 0.7
top_depth = 4.0
eps_value = 1e-06

SIN_PI = tuple(
    math.sqrt(2.0) * term
    for term in (3.1415927410125732, -5.167710304260254, 2.550077438354492, -0.598291277885437, 0.07765766233205795)
)
TINY = 1e-12

HIGHEST = lax.Precision.HIGHEST
VMEM_LIMIT = 24 * 1024 * 1024


def half_turn(turns):
    x = turns - jnp.round(turns)
    square = x * x
    s = SIN_PI[-1]
    for term in SIN_PI[-2::-1]:
        s = s * square + term
    s = s * x
    rest = jnp.maximum(2.0 - s * s, TINY)
    return rest * lax.rsqrt(rest), s, rest - 1.0


def waves(distance, centre_turns, half_step, count):
    c, s, cosine = half_turn(centre_turns * distance)
    amplitude = lax.rsqrt(distance * (1.0 / top_depth))
    mid_c = amplitude * cosine
    mid_s = (amplitude * c) * s
    c, s, step_c = half_turn(half_step * distance)
    step_s = c * s
    cc, ss, cs, sc = mid_c * step_c, mid_s * step_s, mid_c * step_s, mid_s * step_c
    low, high = (cc + ss, sc - cs), (cc - ss, sc + cs)
    lows, highs = [low], [high]
    twice = step_c + step_c
    factor = twice * twice - 2.0
    before_low, before_high = high, low
    for _ in range(count // 2 - 1):
        low, before_low = tuple(factor * a - b for a, b in zip(low, before_low)), low
        high, before_high = tuple(factor * a - b for a, b in zip(high, before_high)), high
        lows.append(low)
        highs.append(high)
    return lows[::-1] + highs


def project_kernel(sizes, part, first, where_ref, foot_ref, basis_ref, after_ref, *refs):
    pos_count, freqs, positions, elements, pos_local, freq_local, foot = sizes
    groups = pos_count // TH
    per_dest = TW // groups
    blocks = elements // ELEM_BLOCK
    steps = pos_local * blocks
    rows = foot * TW
    out_refs, refs = refs[:groups], refs[groups:]
    if first:
        held_ref, refs, sems = refs[0], refs[1:-1], refs[-1]
    else:
        held_ref = basis_ref
    green_even, green_odd, total_ref, depth_ref, lateral_ref, element_ref = refs
    my_pos, my_freq = where_ref[0], where_ref[1]

    def fetch(step):
        offset, block = step // blocks, step % blocks
        spot = pl.ds(block * ELEM_BLOCK, ELEM_BLOCK)
        return pltpu.make_async_copy(basis_ref.at[offset, :, :, spot, :], held_ref.at[step], sems.at[step])

    if first:
        for step in range(steps):
            fetch(step).start()

    cell_row = (my_pos // groups) ^ part
    my_group = lax.rem(my_pos, groups)
    first_freq = (my_freq * freq_local).astype(jnp.float32)
    centre_turns = 0.5 + (first_freq + 0.5 * (freq_local - 1)) / freqs
    half_step = 0.5 / freqs

    row = lax.broadcasted_iota(jnp.int32, (TW, LANES), 0)
    lane = lax.broadcasted_iota(jnp.int32, (TW, LANES), 1)
    cell_col = ((row // per_dest) ^ my_group) * per_dest + row % per_dest
    for offset in range(pos_local):
        pos_global = my_pos * pos_local + offset
        centre = pos_global.astype(jnp.float32) * (cell_spacing * TW * TILE_DEV / positions)
        for piece in range(elements // LANES):
            index = (piece * LANES + lane).astype(jnp.float32)
            element_ref[offset, piece] = (index - 0.5 * (elements - 1)) * elem_pitch + centre

        def place(entry, _, offset=offset, pos_global=pos_global):
            tile = foot_ref[pos_global, entry]
            grid_row = (tile // TILE_DEV) * TH + cell_row
            grid_col = ((tile % TILE_DEV) * TW + cell_col).astype(jnp.float32)
            depth = top_depth + cell_spacing * jnp.full((TW, LANES), grid_row, jnp.int32).astype(jnp.float32)
            depth_ref[offset, entry] = depth * depth
            lateral_ref[offset, entry] = cell_spacing * grid_col
            return 0

        lax.fori_loop(0, foot, place, 0, unroll=4)
    total_ref[...] = jnp.zeros_like(total_ref)

    def green(step, green_ref):
        offset, block = step // blocks, step % blocks
        for pair in range(foot // 2):
            entry = 2 * pair
            depth_square = depth_ref[offset, pl.ds(entry, 2)].reshape(2 * TW, LANES)
            lateral = lateral_ref[offset, pl.ds(entry, 2)].reshape(2 * TW, LANES)
            spot = pl.ds(entry * TW, 2 * TW)
            for sub in range(ELEM_BLOCK // LANES):
                element = element_ref[offset, block * (ELEM_BLOCK // LANES) + sub]
                across = lateral - jnp.concatenate([element, element], axis=0)
                square = depth_square + across * across
                distance = square * lax.rsqrt(square)
                for number, both in enumerate(waves(distance, centre_turns, half_step, freq_local)):
                    for part_of, wave in enumerate(both):
                        start = (number * 2 + part_of) * ELEM_BLOCK + sub * LANES
                        green_ref[spot, start : start + LANES] = wave.astype(jnp.bfloat16)

    def apply(step, green_ref):
        offset = step // blocks
        weights = held_ref[step].reshape(freq_local * 2 * ELEM_BLOCK, -1)
        gain = jnp.dot(green_ref[...], weights, preferred_element_type=jnp.float32)
        for half in range(gain.shape[1] // LANES):
            total_ref[offset, half] = total_ref[offset, half] + gain[:, half * LANES : (half + 1) * LANES]

    def run(make, into, use, out_of):
        if use is not None:
            if first:
                fetch(use).wait()
            apply(use, out_of)
        if make is not None:
            green(make, into)

    run(0, green_even, None, None)

    def two(pair, _):
        run(2 * pair + 1, green_odd, 2 * pair, green_even)
        run(2 * pair + 2, green_even, 2 * pair + 1, green_odd)
        return 0

    lax.fori_loop(0, steps // 2 - 1, two, 0)
    run(steps - 1, green_odd, steps - 2, green_even)
    run(None, None, steps - 1, green_odd)

    for offset in range(pos_local):
        for group in range(groups):
            for cell in range(per_dest):
                for half in range(total_ref.shape[1]):
                    out_refs[group][cell, offset * foot : (offset + 1) * foot, half * LANES : (half + 1) * LANES] = (
                        total_ref[offset, half, pl.ds(group * per_dest + cell, foot, stride=TW), :]
                    )


def project(sizes, part, first, where, footprint, basis, after):
    pos_count, freqs, positions, elements, pos_local, freq_local, foot = sizes
    groups = pos_count // TH
    per_dest = TW // groups
    rank = basis.shape[-1]
    rows = foot * TW
    steps = pos_local * elements // ELEM_BLOCK
    flops = 2 * pos_local * rows * freq_local * 2 * elements * rank
    green = pltpu.VMEM((rows, freq_local * 2 * ELEM_BLOCK), jnp.bfloat16)
    out_shape = [jax.ShapeDtypeStruct((per_dest, pos_local * foot, rank), jnp.float32)] * groups
    if first:
        out_shape.append(jax.ShapeDtypeStruct((steps, freq_local, 2, ELEM_BLOCK, rank), jnp.bfloat16))
    return pl.pallas_call(
        functools.partial(project_kernel, sizes, part, first),
        in_specs=[
            pl.BlockSpec(memory_space=pltpu.SMEM),
            pl.BlockSpec(memory_space=pltpu.SMEM),
            pl.BlockSpec(memory_space=pl.ANY if first else pltpu.VMEM),
            pl.BlockSpec(memory_space=pl.ANY),
        ],
        out_specs=[pl.BlockSpec(memory_space=pltpu.VMEM)] * len(out_shape),
        out_shape=out_shape,
        scratch_shapes=[
            green,
            green,
            pltpu.VMEM((pos_local, rank // LANES, rows, LANES), jnp.float32),
            pltpu.VMEM((pos_local, foot, TW, LANES), jnp.float32),
            pltpu.VMEM((pos_local, foot, TW, LANES), jnp.float32),
            pltpu.VMEM((pos_local, elements // LANES, TW, LANES), jnp.float32),
        ]
        + ([pltpu.SemaphoreType.DMA((steps,))] if first else []),
        compiler_params=pltpu.CompilerParams(vmem_limit_bytes=VMEM_LIMIT),
        cost_estimate=pl.CostEstimate(flops=flops, bytes_accessed=basis.size * 2, transcendentals=0),
        name=f"project_{part}",
    )(where, footprint, basis, after)


def three_terms(values):
    high = values.astype(jnp.bfloat16)
    rest = values - high.astype(jnp.float32)
    mid = rest.astype(jnp.bfloat16)
    return high, mid, (rest - mid.astype(jnp.float32)).astype(jnp.bfloat16)


def gather_kernel(pos_count, freq_count, tile_rows, where_ref, ids_ref, left_ref, right_ref, *refs):
    in_refs, out_refs = refs[:pos_count], refs[pos_count:]
    cells, entries, rank = in_refs[0].shape
    shard = out_refs[0].shape[1]
    tile_cols = shard // tile_rows
    groups = pos_count // TH
    my_pos, my_freq = where_ref[0], where_ref[1]
    left = (lax.rem(my_pos, groups) * 2 >= groups).astype(jnp.int32)
    row = lax.broadcasted_iota(jnp.int32, (shard, entries), 0)
    wanted = (row % tile_rows) * TILE_DEV + row // tile_rows - left
    hot = []
    for other in range(freq_count):
        base = (my_freq ^ other) * (tile_cols - 1)
        col = row // tile_rows - left + base
        hot_row = []
        for source in range(pos_count):
            ids = ids_ref[pl.ds(my_pos ^ source, 1), :]
            hit = (wanted + base == ids) & (col >= 0) & (col < TILE_DEV)
            hot_row.append(hit.astype(jnp.float32).astype(jnp.bfloat16))
        hot_row = jnp.concatenate(hot_row, axis=1)
        hot.append(jnp.concatenate([hot_row] * 3, axis=1))
    for cell in range(cells):
        values = jnp.concatenate([ref[cell] for ref in in_refs], axis=0)
        terms = jnp.concatenate(three_terms(values), axis=0)
        for other in range(freq_count):
            out_refs[other][cell] = jnp.dot(hot[other], terms, preferred_element_type=jnp.float32)


def gather_tiles(freq_count, where, ids, left, right, parts):
    pos_count = len(parts)
    cells, entries, rank = parts[0].shape
    tile_rows = pos_count
    shard = (TILE_DEV // freq_count + 1) * tile_rows
    return pl.pallas_call(
        functools.partial(gather_kernel, pos_count, freq_count, tile_rows),
        in_specs=[pl.BlockSpec(memory_space=pltpu.SMEM), pl.BlockSpec(memory_space=pltpu.VMEM)]
        + [pl.BlockSpec(memory_space=pl.ANY)] * 2
        + [pl.BlockSpec(memory_space=pltpu.VMEM)] * pos_count,
        out_specs=[pl.BlockSpec(memory_space=pltpu.VMEM)] * freq_count,
        out_shape=[jax.ShapeDtypeStruct((cells, shard, rank), jnp.float32)] * freq_count,
        compiler_params=pltpu.CompilerParams(vmem_limit_bytes=VMEM_LIMIT),
        name="tiles",
    )(where, ids, left, right, *parts)


def energy_kernel(freq_count, weights_ref, rims_ref, left_ref, right_ref, *refs):
    in_refs, out_ref = refs[:freq_count], refs[freq_count]
    cells, shard, rank = in_refs[0].shape
    weights = jnp.broadcast_to(weights_ref[...], (8, rank))
    for cell in range(cells):
        summed = in_refs[0][cell]
        for ref in in_refs[1:]:
            summed = summed + ref[cell]
        energy = lax.dot_general(
            weights,
            summed * summed,
            (((1,), (1,)), ((), ())),
            precision=HIGHEST,
            preferred_element_type=jnp.float32,
        )
        out_ref[pl.ds(cell, 1), 0:shard] = jnp.sqrt(energy[0:1] / rank + eps_value)
    rims, edge = rims_ref.shape, left_ref.shape[1]
    out_ref[cells : cells + rims[0], 0 : rims[1]] = rims_ref[...]
    out_ref[cells : cells + rims[0], rims[1] : rims[1] + edge] = right_ref[...]
    out_ref[cells : cells + rims[0], out_ref.shape[1] - edge :] = left_ref[...]


def energies(weights, rims, left, right, shards):
    cells, shard, rank = shards[0].shape
    rows = cells + rims.shape[0]
    width = -(-max(shard, rims.shape[1] + 2 * left.shape[1]) // LANES) * LANES
    return pl.pallas_call(
        functools.partial(energy_kernel, len(shards)),
        in_specs=[pl.BlockSpec(memory_space=pltpu.VMEM)] * (4 + len(shards)),
        out_specs=pl.BlockSpec(memory_space=pltpu.VMEM),
        out_shape=jax.ShapeDtypeStruct((rows, width), jnp.float32),
        compiler_params=pltpu.CompilerParams(vmem_limit_bytes=VMEM_LIMIT),
        name="energies",
    )(weights, rims, left, right, *shards)


def diffuse_kernel(cells, shard, where_ref, strips_ref, out_ref, field_ref):
    pos_count, _, width = strips_ref.shape
    tile_rows = pos_count
    tile_cols = shard // tile_rows
    groups = pos_count // TH
    my_pos = where_ref[0]
    tile_row = lax.broadcasted_iota(jnp.int32, (tile_rows, width), 0)
    spot = lax.broadcasted_iota(jnp.int32, (tile_rows, width), 1)
    here = (spot % tile_rows == tile_row) & (spot < shard)
    source = lax.broadcasted_iota(jnp.int32, (width, LANES), 0)
    target = lax.broadcasted_iota(jnp.int32, (width, LANES), 1)
    field = [jnp.zeros((tile_rows, LANES), jnp.float32) for _ in range(TH)]
    for group in range(groups):
        left = 1 if group * 2 >= groups else 0
        for cell in range(cells):
            col = (source // tile_rows - left) * TW + group * cells + cell
            place = ((target == (col + LANES) % LANES) & (source < shard)).astype(jnp.float32)
            for row in range(TH):
                line = strips_ref[row * groups + group, pl.ds(cell, 1), :]
                spread = jnp.where(here, jnp.broadcast_to(line, (tile_rows, width)), 0.0)
                field[row] = field[row] + jnp.dot(
                    spread, place, precision=HIGHEST, preferred_element_type=jnp.float32
                )

    def strip(which, row):
        return strips_ref[:, cells + which * TH + row, 0:LANES]

    across_k = [strip(0, row) for row in range(TH)]
    along_k = [strip(1, row) for row in range(TH)]
    field = [field[row] + strip(2, row) for row in range(TH)]

    def above(rows, row):
        if row:
            return rows[row - 1]
        return jnp.where(tile_row[:, :LANES] == 0, 0.0, pltpu.roll(rows[TH - 1], 1, 0))

    def below(rows, row):
        if row < TH - 1:
            return rows[row + 1]
        return jnp.where(tile_row[:, :LANES] == tile_rows - 1, 0.0, pltpu.roll(rows[0], tile_rows - 1, 0))

    north_k = [jnp.minimum(across_k[r], above(across_k, r)) for r in range(TH)]
    south_k = [jnp.minimum(across_k[r], below(across_k, r)) for r in range(TH)]
    west_k = [jnp.minimum(k, pltpu.roll(k, 1, 1)) for k in along_k]
    east_k = [jnp.minimum(k, pltpu.roll(k, LANES - 1, 1)) for k in along_k]
    for _ in range(PASSES):
        field = [
            field[r]
            + north_k[r] * (above(field, r) - field[r])
            + south_k[r] * (below(field, r) - field[r])
            + west_k[r] * (pltpu.roll(field[r], 1, 1) - field[r])
            + east_k[r] * (pltpu.roll(field[r], LANES - 1, 1) - field[r])
            for r in range(TH)
        ]
    for row in range(TH):
        field_ref[...] = field[row]
        out_ref[pl.ds(row, 1), :] = field_ref[pl.ds(my_pos, 1), 0 : out_ref.shape[1]]


def diffuse(cells, shard, where, strips, columns):
    return pl.pallas_call(
        functools.partial(diffuse_kernel, cells, shard),
        in_specs=[pl.BlockSpec(memory_space=pltpu.SMEM), pl.BlockSpec(memory_space=pltpu.VMEM)],
        out_specs=pl.BlockSpec(memory_space=pltpu.VMEM),
        out_shape=jax.ShapeDtypeStruct((TH, columns), jnp.float32),
        scratch_shapes=[pltpu.VMEM((strips.shape[0], LANES), jnp.float32)],
        compiler_params=pltpu.CompilerParams(vmem_limit_bytes=VMEM_LIMIT),
        name="diffuse",
    )(where, strips)


def swap(array, axis, distance):
    return lax.ppermute(array, axis, [(i, i ^ distance) for i in range(lax.axis_size(axis))])


def body(footprint, basis, weights, conduct, baseline):
    pos_local, freq_local, doubled, rank = basis.shape
    elements = doubled // 2
    foot = footprint.shape[1]
    pos_count = lax.axis_size("pos")
    freq_count = lax.axis_size("freq")
    columns = baseline.shape[1]
    sizes = (
        pos_count,
        freq_local * freq_count,
        pos_local * pos_count,
        elements,
        pos_local,
        freq_local,
        foot,
    )
    where = jnp.stack([lax.axis_index("pos"), lax.axis_index("freq")]).astype(jnp.int32)
    ids = footprint.reshape(pos_count, pos_local * foot)
    rims = jnp.concatenate([conduct[0], conduct[1], baseline], axis=0)
    left = lax.ppermute(rims[:, columns - TW :], "freq", [(i, i + 1) for i in range(freq_count - 1)])
    right = lax.ppermute(rims[:, :TW], "freq", [(i + 1, i) for i in range(freq_count - 1)])
    split = basis.reshape(pos_local, freq_local, 2, elements, rank)
    groups = pos_count // TH
    parts = [None] * pos_count
    held, after = split, footprint
    for part in range(TH - 1, -1, -1):
        first = part == TH - 1
        sent = list(project(sizes, part, first, where, footprint, held, after))
        held, after = sent.pop() if first else held, sent[0]
        for group in range(groups):
            distance = part * groups + group
            parts[distance] = swap(sent[group], "pos", distance) if distance else sent[group]
    tiles = gather_tiles(freq_count, where, ids, left, right, parts)
    shards = [swap(tiles[d], "freq", d) if d else tiles[d] for d in range(freq_count)]
    strip = energies(weights.reshape(1, rank), rims, left, right, shards)
    strips = lax.all_gather(strip, "pos")
    return diffuse(CELLS // pos_count, shards[0].shape[1], where, strips, columns)


def solution(mesh):
    return jax.shard_map(
        body,
        mesh=mesh,
        in_specs=(P(), P("pos", "freq", None, None), P(), P(None, "pos", "freq"), P("pos", "freq")),
        out_specs=P("pos", "freq"),
        check_vma=False,
    )
```

```python
import functools
import math

import jax
import jax.numpy as jnp
from jax import lax
from jax.experimental import pallas as pl
from jax.experimental.pallas import tpu as pltpu
from jax.sharding import PartitionSpec as P

TH = 4
TW = 8
CELLS = TH * TW
TILE_DEV = 32
PASSES = 3
LANES = 128
ELEM_BLOCK = 256

elem_pitch = 0.125
cell_spacing = 0.7
top_depth = 4.0
eps_value = 1e-06

SIN_PI = tuple(
    math.sqrt(2.0) * term
    for term in (3.1415927410125732, -5.167710304260254, 2.550077438354492, -0.598291277885437, 0.07765766233205795)
)
TINY = 1e-12

HIGHEST = lax.Precision.HIGHEST
VMEM_LIMIT = 24 * 1024 * 1024


def half_turn(turns):
    x = turns - jnp.round(turns)
    square = x * x
    s = SIN_PI[-1]
    for term in SIN_PI[-2::-1]:
        s = s * square + term
    s = s * x
    rest = jnp.maximum(2.0 - s * s, TINY)
    return rest * lax.rsqrt(rest), s, rest - 1.0


def waves(distance, centre_turns, half_step, count):
    c, s, cosine = half_turn(centre_turns * distance)
    amplitude = lax.rsqrt(distance * (1.0 / top_depth))
    mid_c = amplitude * cosine
    mid_s = (amplitude * c) * s
    c, s, step_c = half_turn(half_step * distance)
    step_s = c * s
    cc, ss, cs, sc = mid_c * step_c, mid_s * step_s, mid_c * step_s, mid_s * step_c
    low, high = (cc + ss, sc - cs), (cc - ss, sc + cs)
    lows, highs = [low], [high]
    twice = step_c + step_c
    factor = twice * twice - 2.0
    before_low, before_high = high, low
    for _ in range(count // 2 - 1):
        low, before_low = tuple(factor * a - b for a, b in zip(low, before_low)), low
        high, before_high = tuple(factor * a - b for a, b in zip(high, before_high)), high
        lows.append(low)
        highs.append(high)
    return lows[::-1] + highs


def project_kernel(sizes, part, first, waits, where_ref, foot_ref, basis_ref, *refs):
    pos_count, freqs, positions, elements, pos_local, freq_local, foot = sizes
    groups = pos_count // TH
    per_dest = TW // groups
    blocks = elements // ELEM_BLOCK
    steps = pos_local * blocks
    rows = foot * TW
    out_refs, refs = refs[waits : waits + groups], refs[waits + groups :]
    if first:
        held_ref, refs, sems = refs[0], refs[1:-1], refs[-1]
    else:
        held_ref = basis_ref
    green_even, green_odd, total_ref, depth_ref, lateral_ref, element_ref = refs
    my_pos, my_freq = where_ref[0], where_ref[1]

    def fetch(step):
        offset, block = step // blocks, step % blocks
        spot = pl.ds(block * ELEM_BLOCK, ELEM_BLOCK)
        return pltpu.make_async_copy(basis_ref.at[offset, :, :, spot, :], held_ref.at[step], sems.at[step])

    if first:
        for step in range(steps):
            fetch(step).start()

    cell_row = (my_pos // groups) ^ part
    my_group = lax.rem(my_pos, groups)
    first_freq = (my_freq * freq_local).astype(jnp.float32)
    centre_turns = 0.5 + (first_freq + 0.5 * (freq_local - 1)) / freqs
    half_step = 0.5 / freqs

    row = lax.broadcasted_iota(jnp.int32, (TW, LANES), 0)
    lane = lax.broadcasted_iota(jnp.int32, (TW, LANES), 1)
    cell_col = ((row // per_dest) ^ my_group) * per_dest + row % per_dest
    for offset in range(pos_local):
        pos_global = my_pos * pos_local + offset
        centre = pos_global.astype(jnp.float32) * (cell_spacing * TW * TILE_DEV / positions)
        for piece in range(elements // LANES):
            index = (piece * LANES + lane).astype(jnp.float32)
            element_ref[offset, piece] = (index - 0.5 * (elements - 1)) * elem_pitch + centre

        def place(entry, _, offset=offset, pos_global=pos_global):
            tile = foot_ref[pos_global, entry]
            grid_row = (tile // TILE_DEV) * TH + cell_row
            grid_col = ((tile % TILE_DEV) * TW + cell_col).astype(jnp.float32)
            depth = top_depth + cell_spacing * jnp.full((TW, LANES), grid_row, jnp.int32).astype(jnp.float32)
            depth_ref[offset, entry] = depth * depth
            lateral_ref[offset, entry] = cell_spacing * grid_col
            return 0

        lax.fori_loop(0, foot, place, 0, unroll=4)
    total_ref[...] = jnp.zeros_like(total_ref)

    def green(step, green_ref):
        offset, block = step // blocks, step % blocks
        for pair in range(foot // 2):
            entry = 2 * pair
            depth_square = depth_ref[offset, pl.ds(entry, 2)].reshape(2 * TW, LANES)
            lateral = lateral_ref[offset, pl.ds(entry, 2)].reshape(2 * TW, LANES)
            spot = pl.ds(entry * TW, 2 * TW)
            for sub in range(ELEM_BLOCK // LANES):
                element = element_ref[offset, block * (ELEM_BLOCK // LANES) + sub]
                across = lateral - jnp.concatenate([element, element], axis=0)
                square = depth_square + across * across
                distance = square * lax.rsqrt(square)
                for number, both in enumerate(waves(distance, centre_turns, half_step, freq_local)):
                    for part_of, wave in enumerate(both):
                        start = (number * 2 + part_of) * ELEM_BLOCK + sub * LANES
                        green_ref[spot, start : start + LANES] = wave.astype(jnp.bfloat16)

    def apply(step, green_ref):
        offset = step // blocks
        weights = held_ref[step].reshape(freq_local * 2 * ELEM_BLOCK, -1)
        gain = jnp.dot(green_ref[...], weights, preferred_element_type=jnp.float32)
        for half in range(gain.shape[1] // LANES):
            total_ref[offset, half] = total_ref[offset, half] + gain[:, half * LANES : (half + 1) * LANES]

    def run(make, into, use, out_of):
        if use is not None:
            if first:
                fetch(use).wait()
            apply(use, out_of)
        if make is not None:
            green(make, into)

    run(0, green_even, None, None)

    def two(pair, _):
        run(2 * pair + 1, green_odd, 2 * pair, green_even)
        run(2 * pair + 2, green_even, 2 * pair + 1, green_odd)
        return 0

    lax.fori_loop(0, steps // 2 - 1, two, 0)
    run(steps - 1, green_odd, steps - 2, green_even)
    run(None, None, steps - 1, green_odd)

    for offset in range(pos_local):
        for group in range(groups):
            for cell in range(per_dest):
                for half in range(total_ref.shape[1]):
                    out_refs[group][cell, offset * foot : (offset + 1) * foot, half * LANES : (half + 1) * LANES] = (
                        total_ref[offset, half, pl.ds(group * per_dest + cell, foot, stride=TW), :]
                    )


def project(sizes, part, first, where, footprint, basis, after):
    pos_count, freqs, positions, elements, pos_local, freq_local, foot = sizes
    groups = pos_count // TH
    per_dest = TW // groups
    rank = basis.shape[-1]
    rows = foot * TW
    steps = pos_local * elements // ELEM_BLOCK
    flops = 2 * pos_local * rows * freq_local * 2 * elements * rank
    green = pltpu.VMEM((rows, freq_local * 2 * ELEM_BLOCK), jnp.bfloat16)
    out_shape = [jax.ShapeDtypeStruct((per_dest, pos_local * foot, rank), jnp.float32)] * groups
    if first:
        out_shape.append(jax.ShapeDtypeStruct((steps, freq_local, 2, ELEM_BLOCK, rank), jnp.bfloat16))
    return pl.pallas_call(
        functools.partial(project_kernel, sizes, part, first, len(after)),
        in_specs=[
            pl.BlockSpec(memory_space=pltpu.SMEM),
            pl.BlockSpec(memory_space=pltpu.SMEM),
            pl.BlockSpec(memory_space=pltpu.HBM if first else pltpu.VMEM),
        ]
        + [pl.BlockSpec(memory_space=pl.ANY)] * len(after),
        out_specs=[pl.BlockSpec(memory_space=pltpu.VMEM)] * len(out_shape),
        out_shape=out_shape,
        scratch_shapes=[
            green,
            green,
            pltpu.VMEM((pos_local, rank // LANES, rows, LANES), jnp.float32),
            pltpu.VMEM((pos_local, foot, TW, LANES), jnp.float32),
            pltpu.VMEM((pos_local, foot, TW, LANES), jnp.float32),
            pltpu.VMEM((pos_local, elements // LANES, TW, LANES), jnp.float32),
        ]
        + ([pltpu.SemaphoreType.DMA((steps,))] if first else []),
        compiler_params=pltpu.CompilerParams(vmem_limit_bytes=VMEM_LIMIT),
        cost_estimate=pl.CostEstimate(flops=flops, bytes_accessed=flops, transcendentals=0),
        name=f"project_{part}",
    )(where, footprint, basis, *after)


def three_terms(values):
    high = values.astype(jnp.bfloat16)
    rest = values - high.astype(jnp.float32)
    mid = rest.astype(jnp.bfloat16)
    return high, mid, (rest - mid.astype(jnp.float32)).astype(jnp.bfloat16)


def gather_kernel(pos_count, freq_count, tile_rows, where_ref, ids_ref, *refs):
    in_refs, out_refs = refs[:pos_count], refs[pos_count:]
    cells, entries, rank = in_refs[0].shape
    shard = out_refs[0].shape[1]
    tile_cols = shard // tile_rows
    groups = pos_count // TH
    my_pos, my_freq = where_ref[0], where_ref[1]
    left = (lax.rem(my_pos, groups) * 2 >= groups).astype(jnp.int32)
    row = lax.broadcasted_iota(jnp.int32, (shard, entries), 0)
    wanted = (row % tile_rows) * TILE_DEV + row // tile_rows - left
    hot = []
    for other in range(freq_count):
        base = (my_freq ^ other) * (tile_cols - 1)
        col = row // tile_rows - left + base
        hot_row = []
        for source in range(pos_count):
            ids = ids_ref[pl.ds(my_pos ^ source, 1), :]
            hit = (wanted + base == ids) & (col >= 0) & (col < TILE_DEV)
            hot_row.append(hit.astype(jnp.float32).astype(jnp.bfloat16))
        hot_row = jnp.concatenate(hot_row, axis=1)
        hot.append(jnp.concatenate([hot_row] * 3, axis=1))
    for cell in range(cells):
        values = jnp.concatenate([ref[cell] for ref in in_refs], axis=0)
        terms = jnp.concatenate(three_terms(values), axis=0)
        for other in range(freq_count):
            out_refs[other][cell] = jnp.dot(hot[other], terms, preferred_element_type=jnp.float32)


def gather_tiles(freq_count, where, ids, parts):
    pos_count = len(parts)
    cells, entries, rank = parts[0].shape
    tile_rows = pos_count
    shard = (TILE_DEV // freq_count + 1) * tile_rows
    return pl.pallas_call(
        functools.partial(gather_kernel, pos_count, freq_count, tile_rows),
        in_specs=[pl.BlockSpec(memory_space=pltpu.SMEM), pl.BlockSpec(memory_space=pltpu.VMEM)]
        + [pl.BlockSpec(memory_space=pltpu.VMEM)] * pos_count,
        out_specs=[pl.BlockSpec(memory_space=pltpu.VMEM)] * freq_count,
        out_shape=[jax.ShapeDtypeStruct((cells, shard, rank), jnp.float32)] * freq_count,
        compiler_params=pltpu.CompilerParams(vmem_limit_bytes=VMEM_LIMIT),
        name="tiles",
    )(where, ids, *parts)


def energy_kernel(freq_count, weights_ref, rims_ref, left_ref, right_ref, *refs):
    in_refs, out_ref = refs[:freq_count], refs[freq_count]
    cells, shard, rank = in_refs[0].shape
    weights = jnp.broadcast_to(weights_ref[...], (8, rank))
    for cell in range(cells):
        summed = in_refs[0][cell]
        for ref in in_refs[1:]:
            summed = summed + ref[cell]
        energy = lax.dot_general(
            weights,
            summed * summed,
            (((1,), (1,)), ((), ())),
            precision=HIGHEST,
            preferred_element_type=jnp.float32,
        )
        out_ref[pl.ds(cell, 1), 0:shard] = jnp.sqrt(energy[0:1] / rank + eps_value)
    rims, edge = rims_ref.shape, left_ref.shape[1]
    out_ref[cells : cells + rims[0], 0 : rims[1]] = rims_ref[...]
    out_ref[cells : cells + rims[0], rims[1] : rims[1] + edge] = right_ref[...]
    out_ref[cells : cells + rims[0], out_ref.shape[1] - edge :] = left_ref[...]


def energies(weights, rims, left, right, shards):
    cells, shard, rank = shards[0].shape
    rows = cells + rims.shape[0]
    width = -(-max(shard, rims.shape[1] + 2 * left.shape[1]) // LANES) * LANES
    return pl.pallas_call(
        functools.partial(energy_kernel, len(shards)),
        in_specs=[pl.BlockSpec(memory_space=pltpu.VMEM)] * (4 + len(shards)),
        out_specs=pl.BlockSpec(memory_space=pltpu.VMEM),
        out_shape=jax.ShapeDtypeStruct((rows, width), jnp.float32),
        compiler_params=pltpu.CompilerParams(vmem_limit_bytes=VMEM_LIMIT),
        name="energies",
    )(weights, rims, left, right, *shards)


def diffuse_kernel(cells, shard, where_ref, strips_ref, out_ref, field_ref):
    pos_count, _, width = strips_ref.shape
    tile_rows = pos_count
    tile_cols = shard // tile_rows
    groups = pos_count // TH
    my_pos = where_ref[0]
    tile_row = lax.broadcasted_iota(jnp.int32, (tile_rows, width), 0)
    spot = lax.broadcasted_iota(jnp.int32, (tile_rows, width), 1)
    here = (spot % tile_rows == tile_row) & (spot < shard)
    source = lax.broadcasted_iota(jnp.int32, (width, LANES), 0)
    target = lax.broadcasted_iota(jnp.int32, (width, LANES), 1)
    field = [jnp.zeros((tile_rows, LANES), jnp.float32) for _ in range(TH)]
    for group in range(groups):
        left = 1 if group * 2 >= groups else 0
        for cell in range(cells):
            col = (source // tile_rows - left) * TW + group * cells + cell
            place = ((target == (col + LANES) % LANES) & (source < shard)).astype(jnp.float32)
            for row in range(TH):
                line = strips_ref[row * groups + group, pl.ds(cell, 1), :]
                spread = jnp.where(here, jnp.broadcast_to(line, (tile_rows, width)), 0.0)
                field[row] = field[row] + jnp.dot(
                    spread, place, precision=HIGHEST, preferred_element_type=jnp.float32
                )

    def strip(which, row):
        return strips_ref[:, cells + which * TH + row, 0:LANES]

    across_k = [strip(0, row) for row in range(TH)]
    along_k = [strip(1, row) for row in range(TH)]
    field = [field[row] + strip(2, row) for row in range(TH)]

    def above(rows, row):
        if row:
            return rows[row - 1]
        return jnp.where(tile_row[:, :LANES] == 0, 0.0, pltpu.roll(rows[TH - 1], 1, 0))

    def below(rows, row):
        if row < TH - 1:
            return rows[row + 1]
        return jnp.where(tile_row[:, :LANES] == tile_rows - 1, 0.0, pltpu.roll(rows[0], tile_rows - 1, 0))

    north_k = [jnp.minimum(across_k[r], above(across_k, r)) for r in range(TH)]
    south_k = [jnp.minimum(across_k[r], below(across_k, r)) for r in range(TH)]
    west_k = [jnp.minimum(k, pltpu.roll(k, 1, 1)) for k in along_k]
    east_k = [jnp.minimum(k, pltpu.roll(k, LANES - 1, 1)) for k in along_k]
    for _ in range(PASSES):
        field = [
            field[r]
            + north_k[r] * (above(field, r) - field[r])
            + south_k[r] * (below(field, r) - field[r])
            + west_k[r] * (pltpu.roll(field[r], 1, 1) - field[r])
            + east_k[r] * (pltpu.roll(field[r], LANES - 1, 1) - field[r])
            for r in range(TH)
        ]
    for row in range(TH):
        field_ref[...] = field[row]
        out_ref[pl.ds(row, 1), :] = field_ref[pl.ds(my_pos, 1), 0 : out_ref.shape[1]]


def diffuse(cells, shard, where, strips, columns):
    return pl.pallas_call(
        functools.partial(diffuse_kernel, cells, shard),
        in_specs=[pl.BlockSpec(memory_space=pltpu.SMEM), pl.BlockSpec(memory_space=pltpu.VMEM)],
        out_specs=pl.BlockSpec(memory_space=pltpu.VMEM),
        out_shape=jax.ShapeDtypeStruct((TH, columns), jnp.float32),
        scratch_shapes=[pltpu.VMEM((strips.shape[0], LANES), jnp.float32)],
        compiler_params=pltpu.CompilerParams(vmem_limit_bytes=VMEM_LIMIT),
        name="diffuse",
    )(where, strips)


def swap(array, axis, distance):
    return lax.ppermute(array, axis, [(i, i ^ distance) for i in range(lax.axis_size(axis))])


def body(footprint, basis, weights, conduct, baseline):
    pos_local, freq_local, doubled, rank = basis.shape
    elements = doubled // 2
    foot = footprint.shape[1]
    pos_count = lax.axis_size("pos")
    freq_count = lax.axis_size("freq")
    columns = baseline.shape[1]
    sizes = (
        pos_count,
        freq_local * freq_count,
        pos_local * pos_count,
        elements,
        pos_local,
        freq_local,
        foot,
    )
    where = jnp.stack([lax.axis_index("pos"), lax.axis_index("freq")]).astype(jnp.int32)
    ids = footprint.reshape(pos_count, pos_local * foot)
    rims = jnp.concatenate([conduct[0], conduct[1], baseline], axis=0)
    left = lax.ppermute(rims[:, columns - TW :], "freq", [(i, i + 1) for i in range(freq_count - 1)])
    right = lax.ppermute(rims[:, :TW], "freq", [(i + 1, i) for i in range(freq_count - 1)])
    split = basis.reshape(pos_local, freq_local, 2, elements, rank)
    groups = pos_count // TH
    parts = [None] * pos_count
    held, after = split, ()
    for part in range(TH - 1, -1, -1):
        first = part == TH - 1
        sent = list(project(sizes, part, first, where, footprint, held, after))
        held = sent.pop() if first else held
        for group in range(groups):
            distance = part * groups + group
            parts[distance] = swap(sent[group], "pos", distance) if distance else sent[group]
        after = (sent[0],)
        if first:
            after += (left, right)
        if part == 1:
            after += tuple(parts[-groups:])
    tiles = gather_tiles(freq_count, where, ids, parts)
    shards = [swap(tiles[d], "freq", d) if d else tiles[d] for d in range(freq_count)]
    strip = energies(weights.reshape(1, rank), rims, left, right, shards)
    strips = lax.all_gather(strip, "pos")
    return diffuse(CELLS // pos_count, shards[0].shape[1], where, strips, columns)


def solution(mesh):
    return jax.shard_map(
        body,
        mesh=mesh,
        in_specs=(P(), P("pos", "freq", None, None), P(), P(None, "pos", "freq"), P("pos", "freq")),
        out_specs=P("pos", "freq"),
        check_vma=False,
    )
```

```python
import functools
import math

import jax
import jax.numpy as jnp
from jax import lax
from jax.experimental import pallas as pl
from jax.experimental.pallas import tpu as pltpu
from jax.sharding import PartitionSpec as P

TH = 4
TW = 8
CELLS = TH * TW
TILE_DEV = 32
PASSES = 3
LANES = 128
ELEM_BLOCK = 256

elem_pitch = 0.125
cell_spacing = 0.7
top_depth = 4.0
eps_value = 1e-06

SIN_PI = tuple(
    math.sqrt(2.0) * (1.0 - 2e-6) * term
    for term in (3.1415903568267822, -5.1674065589904785, 2.5440104007720947, -0.5594624280929565)
)

HIGHEST = lax.Precision.HIGHEST
VMEM_LIMIT = 24 * 1024 * 1024
VMEM_LIMIT_FIRST = 42 * 1024 * 1024


def half_turn(turns):
    x = turns - jnp.round(turns)
    square = x * x
    s = SIN_PI[-1]
    for term in SIN_PI[-2::-1]:
        s = s * square + term
    s = s * x
    rest = 2.0 - s * s
    return rest * lax.rsqrt(rest), s, rest - 1.0


def waves(distance, first_turns, step_turns, count):
    c, s, cosine = half_turn(first_turns * distance)
    amplitude = lax.rsqrt(distance)
    last = amplitude * cosine, (amplitude * c) * s
    c, s, cosine = half_turn(step_turns * distance)
    sine = c * s
    now = last[0] * cosine - last[1] * sine, last[1] * cosine + last[0] * sine
    found = [last, now]
    twice = cosine + cosine
    for _ in range(count - 2):
        now, last = tuple(twice * a - b for a, b in zip(now, last)), now
        found.append(now)
    return found[:count]


def project_kernel(sizes, part, first, waits, *refs):
    pos_count, freqs, positions, elements, pos_local, freq_local, foot = sizes
    groups = pos_count // TH
    per_dest = TW // groups
    blocks = elements // ELEM_BLOCK
    steps = pos_local * blocks
    where_ref, refs = refs[0], refs[1:]
    if first:
        (foot_ref, basis_ref, conduct_ref, baseline_ref), refs = refs[:4], refs[4:]
        out_refs, refs = refs[:groups], refs[groups:]
        held_ref, depth_ref, lateral_ref, element_ref, rims_ref, head_ref, tail_ref = refs[:7]
        green_even, green_odd, total_ref, sems = refs[7:]
    else:
        held_ref, depth_ref, lateral_ref, element_ref = refs[:4]
        out_refs, refs = refs[4 + waits : 4 + waits + groups], refs[4 + waits + groups :]
        green_even, green_odd, total_ref = refs
    my_pos, my_freq = where_ref[0], where_ref[1]

    def fetch(step):
        offset, block = step // blocks, step % blocks
        spot = pl.ds(block * ELEM_BLOCK, ELEM_BLOCK)
        return pltpu.make_async_copy(basis_ref.at[offset, :, :, spot, :], held_ref.at[step], sems.at[step])

    if first:
        for step in range(steps):
            fetch(step).start()

    first_freq = (my_freq * freq_local).astype(jnp.float32)
    first_turns = top_depth * (0.5 + first_freq / freqs)
    step_turns = top_depth / freqs

    if first:
        scale = 1.0 / top_depth
        my_group = lax.rem(my_pos, groups)
        row = lax.broadcasted_iota(jnp.int32, (TW, LANES), 0)
        lane = lax.broadcasted_iota(jnp.int32, (TW, LANES), 1)
        cell_col = ((row // per_dest) ^ my_group) * per_dest + row % per_dest
        for offset in range(pos_local):
            pos_global = my_pos * pos_local + offset
            centre = pos_global.astype(jnp.float32) * (cell_spacing * TW * TILE_DEV / positions)
            for piece in range(elements // LANES):
                index = (piece * LANES + lane).astype(jnp.float32)
                element_ref[offset, piece] = scale * ((index - 0.5 * (elements - 1)) * elem_pitch + centre)

            def place(entry, _, offset=offset, pos_global=pos_global):
                tile = foot_ref[pos_global, entry]
                for other in range(TH):
                    grid_row = (tile // TILE_DEV) * TH + ((my_pos // groups) ^ other)
                    depth = scale * (top_depth + cell_spacing * jnp.full((TW, LANES), grid_row, jnp.int32).astype(jnp.float32))
                    depth_ref[other, offset, entry] = depth * depth
                grid_col = ((tile % TILE_DEV) * TW + cell_col).astype(jnp.float32)
                lateral_ref[offset, entry] = scale * (cell_spacing * grid_col)
                return 0

            lax.fori_loop(0, foot, place, 0, unroll=8)
        columns = rims_ref.shape[1]
        for number, block in enumerate((conduct_ref[0], conduct_ref[1], baseline_ref[...])):
            span = slice(number * TH, (number + 1) * TH)
            rims_ref[span, :] = block
            head_ref[span, :] = block[:, :TW]
            tail_ref[span, :] = block[:, columns - TW :]
    total_ref[...] = jnp.zeros_like(total_ref)

    def green(step, green_ref):
        offset, block = step // blocks, step % blocks
        for pair in range(foot // 2):
            entry = 2 * pair
            depth_square = depth_ref[part, offset, pl.ds(entry, 2)].reshape(2 * TW, LANES)
            lateral = lateral_ref[offset, pl.ds(entry, 2)].reshape(2 * TW, LANES)
            spot = pl.ds(entry * TW, 2 * TW)
            for sub in range(ELEM_BLOCK // LANES):
                element = element_ref[offset, block * (ELEM_BLOCK // LANES) + sub]
                across = lateral - jnp.concatenate([element, element], axis=0)
                square = depth_square + across * across
                distance = square * lax.rsqrt(square)
                for number, both in enumerate(waves(distance, first_turns, step_turns, freq_local)):
                    for part_of, wave in enumerate(both):
                        start = (number * 2 + part_of) * ELEM_BLOCK + sub * LANES
                        green_ref[spot, start : start + LANES] = wave.astype(jnp.bfloat16)

    def apply(step, green_ref):
        offset = step // blocks
        weights = held_ref[step].reshape(freq_local * 2 * ELEM_BLOCK, -1)
        gain = jnp.dot(green_ref[...], weights, preferred_element_type=jnp.float32)
        for half in range(gain.shape[1] // LANES):
            total_ref[offset, half] = total_ref[offset, half] + gain[:, half * LANES : (half + 1) * LANES]

    def run(make, into, use, out_of):
        if use is not None:
            if first:
                fetch(use).wait()
            apply(use, out_of)
        if make is not None:
            green(make, into)

    run(0, green_even, None, None)

    def two(pair, _):
        run(2 * pair + 1, green_odd, 2 * pair, green_even)
        run(2 * pair + 2, green_even, 2 * pair + 1, green_odd)
        return 0

    lax.fori_loop(0, steps // 2 - 1, two, 0)
    run(steps - 1, green_odd, steps - 2, green_even)
    run(None, None, steps - 1, green_odd)

    for offset in range(pos_local):
        for group in range(groups):
            for cell in range(per_dest):
                for half in range(total_ref.shape[1]):
                    out_refs[group][cell, offset * foot : (offset + 1) * foot, half * LANES : (half + 1) * LANES] = (
                        total_ref[offset, half, pl.ds(group * per_dest + cell, foot, stride=TW), :]
                    )


def project(sizes, part, first, operands, after):
    pos_count, freqs, positions, elements, pos_local, freq_local, foot = sizes
    groups = pos_count // TH
    per_dest = TW // groups
    basis = operands[2] if first else operands[1]
    rank = basis.shape[-1]
    rows = foot * TW
    steps = pos_local * elements // ELEM_BLOCK
    flops = 2 * pos_local * rows * freq_local * 2 * elements * rank

    def shape(*dims, dtype=jnp.float32):
        return jax.ShapeDtypeStruct(dims, dtype)

    vmem, smem = pl.BlockSpec(memory_space=pltpu.VMEM), pl.BlockSpec(memory_space=pltpu.SMEM)
    out_shape = [shape(per_dest, pos_local * foot, rank)] * groups
    if first:
        in_specs = [smem, smem, pl.BlockSpec(memory_space=pl.ANY), vmem, vmem]
        columns = operands[4].shape[1]
        out_shape += [
            shape(steps, freq_local, 2, ELEM_BLOCK, rank, dtype=jnp.bfloat16),
            shape(TH, pos_local, foot, TW, LANES),
            shape(pos_local, foot, TW, LANES),
            shape(pos_local, elements // LANES, TW, LANES),
            shape(3 * TH, columns),
            shape(3 * TH, TW),
            shape(3 * TH, TW),
        ]
    else:
        in_specs = [smem] + [vmem] * 4 + [pl.BlockSpec(memory_space=pl.ANY)] * len(after)
    green = pltpu.VMEM((rows, freq_local * 2 * ELEM_BLOCK), jnp.bfloat16)
    return pl.pallas_call(
        functools.partial(project_kernel, sizes, part, first, len(after)),
        in_specs=in_specs,
        out_specs=[vmem] * len(out_shape),
        out_shape=out_shape,
        scratch_shapes=[green, green, pltpu.VMEM((pos_local, rank // LANES, rows, LANES), jnp.float32)]
        + ([pltpu.SemaphoreType.DMA((steps,))] if first else []),
        compiler_params=pltpu.CompilerParams(vmem_limit_bytes=VMEM_LIMIT_FIRST if first else VMEM_LIMIT),
        cost_estimate=pl.CostEstimate(flops=flops, bytes_accessed=flops, transcendentals=0),
        name=f"project_{part}",
    )(*operands, *after)


def two_terms(values):
    high = values.astype(jnp.bfloat16)
    return high, (values - high.astype(jnp.float32)).astype(jnp.bfloat16)


def gather_kernel(pos_count, freq_count, tile_rows, where_ref, ids_ref, *refs):
    in_refs, out_refs = refs[:pos_count], refs[pos_count:]
    cells, entries, rank = in_refs[0].shape
    shard = out_refs[0].shape[1]
    tile_cols = shard // tile_rows
    groups = pos_count // TH
    my_pos, my_freq = where_ref[0], where_ref[1]
    left = (lax.rem(my_pos, groups) * 2 >= groups).astype(jnp.int32)
    row = lax.broadcasted_iota(jnp.int32, (shard, entries), 0)
    wanted = (row % tile_rows) * TILE_DEV + row // tile_rows - left
    hot = []
    for other in range(freq_count):
        base = (my_freq ^ other) * (tile_cols - 1)
        col = row // tile_rows - left + base
        hot_row = []
        for source in range(pos_count):
            ids = ids_ref[pl.ds(my_pos ^ source, 1), :]
            hit = (wanted + base == ids) & (col >= 0) & (col < TILE_DEV)
            hot_row.append(hit.astype(jnp.float32).astype(jnp.bfloat16))
        hot_row = jnp.concatenate(hot_row, axis=1)
        hot.append(jnp.concatenate([hot_row] * 2, axis=1))
    for cell in range(cells):
        values = jnp.concatenate([ref[cell] for ref in in_refs], axis=0)
        terms = jnp.concatenate(two_terms(values), axis=0)
        for other in range(freq_count):
            out_refs[other][cell] = jnp.dot(hot[other], terms, preferred_element_type=jnp.float32)


def gather_tiles(freq_count, where, ids, parts):
    pos_count = len(parts)
    cells, entries, rank = parts[0].shape
    tile_rows = pos_count
    shard = (TILE_DEV // freq_count + 1) * tile_rows
    return pl.pallas_call(
        functools.partial(gather_kernel, pos_count, freq_count, tile_rows),
        in_specs=[pl.BlockSpec(memory_space=pltpu.SMEM), pl.BlockSpec(memory_space=pltpu.VMEM)]
        + [pl.BlockSpec(memory_space=pltpu.VMEM)] * pos_count,
        out_specs=[pl.BlockSpec(memory_space=pltpu.VMEM)] * freq_count,
        out_shape=[jax.ShapeDtypeStruct((cells, shard, rank), jnp.float32)] * freq_count,
        compiler_params=pltpu.CompilerParams(vmem_limit_bytes=VMEM_LIMIT),
        name="tiles",
    )(where, ids, *parts)


def energy_kernel(freq_count, weights_ref, rims_ref, left_ref, right_ref, *refs):
    in_refs, out_ref = refs[:freq_count], refs[freq_count]
    cells, shard, rank = in_refs[0].shape
    weights = jnp.broadcast_to(weights_ref[...], (8, rank))
    for cell in range(cells):
        summed = in_refs[0][cell]
        for ref in in_refs[1:]:
            summed = summed + ref[cell]
        energy = lax.dot_general(
            weights,
            summed * summed,
            (((1,), (1,)), ((), ())),
            precision=HIGHEST,
            preferred_element_type=jnp.float32,
        )
        out_ref[pl.ds(cell, 1), 0:shard] = jnp.sqrt(energy[0:1] / rank + eps_value)
    rims, edge = rims_ref.shape, left_ref.shape[1]
    out_ref[cells : cells + rims[0], 0 : rims[1]] = rims_ref[...]
    out_ref[cells : cells + rims[0], rims[1] : rims[1] + edge] = right_ref[...]
    out_ref[cells : cells + rims[0], out_ref.shape[1] - edge :] = left_ref[...]


def energies(weights, rims, left, right, shards):
    cells, shard, rank = shards[0].shape
    rows = cells + rims.shape[0]
    width = -(-max(shard, rims.shape[1] + 2 * left.shape[1]) // LANES) * LANES
    return pl.pallas_call(
        functools.partial(energy_kernel, len(shards)),
        in_specs=[pl.BlockSpec(memory_space=pltpu.VMEM)] * (4 + len(shards)),
        out_specs=pl.BlockSpec(memory_space=pltpu.VMEM),
        out_shape=jax.ShapeDtypeStruct((rows, width), jnp.float32),
        compiler_params=pltpu.CompilerParams(vmem_limit_bytes=VMEM_LIMIT),
        name="energies",
    )(weights, rims, left, right, *shards)


def diffuse_kernel(cells, shard, where_ref, strips_ref, out_ref, field_ref):
    pos_count, _, width = strips_ref.shape
    tile_rows = pos_count
    tile_cols = shard // tile_rows
    groups = pos_count // TH
    my_pos = where_ref[0]
    tile_row = lax.broadcasted_iota(jnp.int32, (tile_rows, width), 0)
    spot = lax.broadcasted_iota(jnp.int32, (tile_rows, width), 1)
    here = (spot % tile_rows == tile_row) & (spot < shard)
    source = lax.broadcasted_iota(jnp.int32, (width, LANES), 0)
    target = lax.broadcasted_iota(jnp.int32, (width, LANES), 1)
    field = jnp.zeros((TH * tile_rows, LANES), jnp.float32)
    for group in range(groups):
        left = 1 if group * 2 >= groups else 0
        for cell in range(cells):
            col = (source // tile_rows - left) * TW + group * cells + cell
            place = ((target == (col + LANES) % LANES) & (source < shard)).astype(jnp.float32)
            spread = []
            for row in range(TH):
                line = strips_ref[row * groups + group, pl.ds(cell, 1), :]
                spread.append(jnp.where(here, jnp.broadcast_to(line, (tile_rows, width)), 0.0))
            field = field + jnp.dot(
                jnp.concatenate(spread, axis=0), place, precision=HIGHEST, preferred_element_type=jnp.float32
            )

    def strip(which, row):
        return strips_ref[:, cells + which * TH + row, 0:LANES]

    across_k = [strip(0, row) for row in range(TH)]
    along_k = [strip(1, row) for row in range(TH)]
    field = [field[row * tile_rows : (row + 1) * tile_rows] + strip(2, row) for row in range(TH)]

    def above(rows, row):
        if row:
            return rows[row - 1]
        return jnp.where(tile_row[:, :LANES] == 0, 0.0, pltpu.roll(rows[TH - 1], 1, 0))

    def below(rows, row):
        if row < TH - 1:
            return rows[row + 1]
        return jnp.where(tile_row[:, :LANES] == tile_rows - 1, 0.0, pltpu.roll(rows[0], tile_rows - 1, 0))

    north_k = [jnp.minimum(across_k[r], above(across_k, r)) for r in range(TH)]
    south_k = [jnp.minimum(across_k[r], below(across_k, r)) for r in range(TH)]
    west_k = [jnp.minimum(k, pltpu.roll(k, 1, 1)) for k in along_k]
    east_k = [jnp.minimum(k, pltpu.roll(k, LANES - 1, 1)) for k in along_k]
    for _ in range(PASSES):
        field = [
            field[r]
            + north_k[r] * (above(field, r) - field[r])
            + south_k[r] * (below(field, r) - field[r])
            + west_k[r] * (pltpu.roll(field[r], 1, 1) - field[r])
            + east_k[r] * (pltpu.roll(field[r], LANES - 1, 1) - field[r])
            for r in range(TH)
        ]
    for row in range(TH):
        field_ref[...] = field[row]
        out_ref[pl.ds(row, 1), :] = field_ref[pl.ds(my_pos, 1), 0 : out_ref.shape[1]]


def diffuse(cells, shard, where, strips, columns):
    return pl.pallas_call(
        functools.partial(diffuse_kernel, cells, shard),
        in_specs=[pl.BlockSpec(memory_space=pltpu.SMEM), pl.BlockSpec(memory_space=pltpu.VMEM)],
        out_specs=pl.BlockSpec(memory_space=pltpu.VMEM),
        out_shape=jax.ShapeDtypeStruct((TH, columns), jnp.float32),
        scratch_shapes=[pltpu.VMEM((strips.shape[0], LANES), jnp.float32)],
        compiler_params=pltpu.CompilerParams(vmem_limit_bytes=VMEM_LIMIT),
        name="diffuse",
    )(where, strips)


def swap(array, axis, distance):
    return lax.ppermute(array, axis, [(i, i ^ distance) for i in range(lax.axis_size(axis))])


def body(footprint, basis, weights, conduct, baseline):
    pos_local, freq_local, doubled, rank = basis.shape
    elements = doubled // 2
    foot = footprint.shape[1]
    pos_count = lax.axis_size("pos")
    freq_count = lax.axis_size("freq")
    columns = baseline.shape[1]
    sizes = (
        pos_count,
        freq_local * freq_count,
        pos_local * pos_count,
        elements,
        pos_local,
        freq_local,
        foot,
    )
    where = jnp.stack([lax.axis_index("pos"), lax.axis_index("freq")]).astype(jnp.int32)
    ids = footprint.reshape(pos_count, pos_local * foot)
    split = basis.reshape(pos_local, freq_local, 2, elements, rank)
    groups = pos_count // TH
    parts = [None] * pos_count
    operands, after = (where, footprint, split, conduct, baseline), ()
    for part in range(TH - 1, -1, -1):
        first = part == TH - 1
        sent = project(sizes, part, first, operands, after)
        for group in range(groups):
            distance = part * groups + group
            parts[distance] = swap(sent[group], "pos", distance) if distance else sent[group]
        after = (sent[0],)
        if first:
            held, depth, lateral, element, rims, head, tail = sent[groups:]
            operands = where, held, depth, lateral, element
            left = lax.ppermute(tail, "freq", [(i, i + 1) for i in range(freq_count - 1)])
            right = lax.ppermute(head, "freq", [(i + 1, i) for i in range(freq_count - 1)])
        if part == 2:
            after += (left, right)
        if part == 1:
            after += tuple(parts[-groups:])
    tiles = gather_tiles(freq_count, where, ids, parts)
    shards = [swap(tiles[d], "freq", d) if d else tiles[d] for d in range(freq_count)]
    strip = energies(weights.reshape(1, rank), rims, left, right, shards)
    strips = lax.all_gather(strip, "pos")
    return diffuse(CELLS // pos_count, shards[0].shape[1], where, strips, columns)


def solution(mesh):
    return jax.shard_map(
        body,
        mesh=mesh,
        in_specs=(P(), P("pos", "freq", None, None), P(), P(None, "pos", "freq"), P("pos", "freq")),
        out_specs=P("pos", "freq"),
        check_vma=False,
    )
```

```python
import functools
import math

import jax
import jax.numpy as jnp
from jax import lax
from jax.experimental import pallas as pl
from jax.experimental.pallas import tpu as pltpu
from jax.sharding import PartitionSpec as P

TH = 4
TW = 8
CELLS = TH * TW
TILE_DEV = 32
PASSES = 3
LANES = 128
RIM_ROWS = 8
ELEM_BLOCK = 256
AHEAD = 3

elem_pitch = 0.125
cell_spacing = 0.7
top_depth = 4.0
eps_value = 1e-06

SIN_PI = tuple(
    math.sqrt(2.0) * (1.0 - 2e-6) * term
    for term in (3.1415903568267822, -5.1674065589904785, 2.5440104007720947, -0.5594624280929565)
)

HIGHEST = lax.Precision.HIGHEST
VMEM_LIMIT = 24 * 1024 * 1024
VMEM_LIMIT_FIRST = 42 * 1024 * 1024


def half_turn(turns):
    x = turns - jnp.round(turns)
    square = x * x
    s = SIN_PI[-1]
    for term in SIN_PI[-2::-1]:
        s = s * square + term
    s = s * x
    rest = 2.0 - s * s
    return rest * lax.rsqrt(rest), s, rest - 1.0


def waves(distance, first_turns, step_turns, count):
    c, s, cosine = half_turn(first_turns * distance)
    amplitude = lax.rsqrt(distance)
    last = amplitude * cosine, (amplitude * c) * s
    c, s, cosine = half_turn(step_turns * distance)
    sine = c * s
    now = last[0] * cosine - last[1] * sine, last[1] * cosine + last[0] * sine
    found = [last, now]
    twice = cosine + cosine
    for _ in range(count - 2):
        now, last = tuple(twice * a - b for a, b in zip(now, last)), now
        found.append(now)
    return found[:count]


def project_kernel(sizes, rounds, turn, waits, *refs):
    first = turn == 0
    pos_count, freqs, positions, elements, pos_local, freq_local, foot = sizes
    groups = pos_count // TH
    per_dest = TW // groups
    blocks = elements // ELEM_BLOCK
    steps = pos_local * blocks
    where_ref, refs = refs[0], refs[1:]
    if first:
        (foot_ref, basis_ref), refs = refs[:2], refs[2:]
        out_refs, refs = refs[:groups], refs[groups:]
        held_ref, depth_ref, lateral_ref, element_ref, green_even, green_odd, total_ref, sems = refs
    else:
        held_ref, depth_ref, lateral_ref, element_ref = refs[:4]
        out_refs, refs = refs[4 + waits : 4 + waits + groups], refs[4 + waits + groups :]
        green_even, green_odd, total_ref = refs
    my_pos, my_freq = where_ref[0], where_ref[1]

    def fetch(step):
        offset, block = step // blocks, step % blocks
        spot = pl.ds(block * ELEM_BLOCK, ELEM_BLOCK)
        return pltpu.make_async_copy(basis_ref.at[offset, :, :, spot, :], held_ref.at[step], sems.at[step])

    if first:
        for step in range(AHEAD):
            fetch(step).start()

    first_freq = (my_freq * freq_local).astype(jnp.float32)
    first_turns = top_depth * (0.5 + first_freq / freqs)
    step_turns = top_depth / freqs

    if first:
        scale = 1.0 / top_depth
        row = lax.broadcasted_iota(jnp.int32, (TW, LANES), 0)
        lane = lax.broadcasted_iota(jnp.int32, (TW, LANES), 1)
        places = []
        for distances in rounds:
            target = my_pos ^ functools.reduce(
                lambda rest, here: jnp.where(row // per_dest == here, distances[here], rest), range(1, groups), distances[0]
            )
            places.append((target // groups, (target % groups) * per_dest + row % per_dest))
        for offset in range(pos_local):
            pos_global = my_pos * pos_local + offset
            centre = pos_global.astype(jnp.float32) * (cell_spacing * TW * TILE_DEV / positions)
            for piece in range(elements // LANES):
                index = (piece * LANES + lane).astype(jnp.float32)
                element_ref[offset, piece] = scale * ((index - 0.5 * (elements - 1)) * elem_pitch + centre)

            def place(entry, _, offset=offset, pos_global=pos_global):
                tile = foot_ref[pos_global, entry]
                for number, (cell_row, cell_col) in enumerate(places):
                    grid_row = ((tile // TILE_DEV) * TH + cell_row).astype(jnp.float32)
                    grid_col = ((tile % TILE_DEV) * TW + cell_col).astype(jnp.float32)
                    depth = scale * (top_depth + cell_spacing * grid_row)
                    depth_ref[number, offset, entry] = depth * depth
                    lateral_ref[number, offset, entry] = scale * (cell_spacing * grid_col)
                return 0

            lax.fori_loop(0, foot, place, 0, unroll=4)
    total_ref[...] = jnp.zeros_like(total_ref)

    def green(step, green_ref):
        offset, block = step // blocks, step % blocks
        for pair in range(foot // 2):
            entry = 2 * pair
            depth_square = depth_ref[turn, offset, pl.ds(entry, 2)].reshape(2 * TW, LANES)
            lateral = lateral_ref[turn, offset, pl.ds(entry, 2)].reshape(2 * TW, LANES)
            spot = pl.ds(entry * TW, 2 * TW)
            for sub in range(ELEM_BLOCK // LANES):
                element = element_ref[offset, block * (ELEM_BLOCK // LANES) + sub]
                across = lateral - jnp.concatenate([element, element], axis=0)
                square = depth_square + across * across
                distance = square * lax.rsqrt(square)
                for number, both in enumerate(waves(distance, first_turns, step_turns, freq_local)):
                    for part_of, wave in enumerate(both):
                        start = (number * 2 + part_of) * ELEM_BLOCK + sub * LANES
                        green_ref[spot, start : start + LANES] = wave.astype(jnp.bfloat16)

    def apply(step, green_ref):
        offset = step // blocks
        weights = held_ref[step].reshape(freq_local * 2 * ELEM_BLOCK, -1)
        gain = jnp.dot(green_ref[...], weights, preferred_element_type=jnp.float32)
        for half in range(gain.shape[1] // LANES):
            total_ref[offset, half] = total_ref[offset, half] + gain[:, half * LANES : (half + 1) * LANES]

    def run(make, into, use, out_of):
        if use is not None:
            if first:
                fetch(use).wait()
                if isinstance(use, int):
                    if use + AHEAD < steps:
                        fetch(use + AHEAD).start()
                else:
                    pl.when(use + AHEAD < steps)(lambda: fetch(use + AHEAD).start())
            apply(use, out_of)
        if make is not None:
            green(make, into)

    run(0, green_even, None, None)

    def two(pair, _):
        run(2 * pair + 1, green_odd, 2 * pair, green_even)
        run(2 * pair + 2, green_even, 2 * pair + 1, green_odd)
        return 0

    lax.fori_loop(0, steps // 2 - 1, two, 0)
    run(steps - 1, green_odd, steps - 2, green_even)
    run(None, None, steps - 1, green_odd)

    for offset in range(pos_local):
        for group in range(groups):
            for cell in range(per_dest):
                for half in range(total_ref.shape[1]):
                    out_refs[group][cell, offset * foot : (offset + 1) * foot, half * LANES : (half + 1) * LANES] = (
                        total_ref[offset, half, pl.ds(group * per_dest + cell, foot, stride=TW), :]
                    )


def project(sizes, rounds, turn, operands, after):
    first = turn == 0
    pos_count, freqs, positions, elements, pos_local, freq_local, foot = sizes
    groups = pos_count // TH
    per_dest = TW // groups
    basis = operands[2] if first else operands[1]
    rank = basis.shape[-1]
    rows = foot * TW
    steps = pos_local * elements // ELEM_BLOCK
    flops = 2 * pos_local * rows * freq_local * 2 * elements * rank

    def shape(*dims, dtype=jnp.float32):
        return jax.ShapeDtypeStruct(dims, dtype)

    vmem, smem = pl.BlockSpec(memory_space=pltpu.VMEM), pl.BlockSpec(memory_space=pltpu.SMEM)
    out_shape = [shape(per_dest, pos_local * foot, rank)] * groups
    if first:
        in_specs = [smem, smem, pl.BlockSpec(memory_space=pl.ANY)]
        out_shape += [
            shape(steps, freq_local, 2, ELEM_BLOCK, rank, dtype=jnp.bfloat16),
            shape(len(rounds), pos_local, foot, TW, LANES),
            shape(len(rounds), pos_local, foot, TW, LANES),
            shape(pos_local, elements // LANES, TW, LANES),
        ]
    else:
        in_specs = [smem] + [vmem] * 4 + [pl.BlockSpec(memory_space=pl.ANY)] * len(after)
    green = pltpu.VMEM((rows, freq_local * 2 * ELEM_BLOCK), jnp.bfloat16)
    return pl.pallas_call(
        functools.partial(project_kernel, sizes, rounds, turn, len(after)),
        in_specs=in_specs,
        out_specs=[vmem] * len(out_shape),
        out_shape=out_shape,
        scratch_shapes=[green, green, pltpu.VMEM((pos_local, rank // LANES, rows, LANES), jnp.float32)]
        + ([pltpu.SemaphoreType.DMA((steps,))] if first else []),
        compiler_params=pltpu.CompilerParams(vmem_limit_bytes=VMEM_LIMIT_FIRST if first else VMEM_LIMIT),
        cost_estimate=pl.CostEstimate(flops=flops, bytes_accessed=flops, transcendentals=0),
        name=f"project_{turn}",
    )(*operands, *after)


def two_terms(values):
    high = values.astype(jnp.bfloat16)
    return high, (values - high.astype(jnp.float32)).astype(jnp.bfloat16)


def gather_kernel(pos_count, freq_count, tile_rows, shard, where_ref, ids_ref, conduct_ref, baseline_ref, *refs):
    in_refs, out_refs = refs[:pos_count], refs[pos_count:]
    cells, entries, rank = in_refs[0].shape
    columns = baseline_ref.shape[1]
    tile_cols = shard // tile_rows
    groups = pos_count // TH
    my_pos, my_freq = where_ref[0], where_ref[1]
    left = (lax.rem(my_pos, groups) * 2 >= groups).astype(jnp.int32)
    row = lax.broadcasted_iota(jnp.int32, (shard, entries), 0)
    wanted = (row % tile_rows) * TILE_DEV + row // tile_rows - left
    hot = []
    for other in range(freq_count):
        base = (my_freq ^ other) * (tile_cols - 1)
        col = row // tile_rows - left + base
        hot_row = []
        for source in range(pos_count):
            ids = ids_ref[pl.ds(my_pos ^ source, 1), :]
            hit = (wanted + base == ids) & (col >= 0) & (col < TILE_DEV)
            hot_row.append(hit.astype(jnp.float32).astype(jnp.bfloat16))
        hot_row = jnp.concatenate(hot_row, axis=1)
        hot.append(jnp.concatenate([hot_row] * 2, axis=1))
    for cell in range(cells):
        values = jnp.concatenate([ref[cell] for ref in in_refs], axis=0)
        terms = jnp.concatenate(two_terms(values), axis=0)
        for other in range(freq_count):
            span = slice(cell * shard, (cell + 1) * shard)
            out_refs[other][span, :] = jnp.dot(hot[other], terms, preferred_element_type=jnp.float32)
    last = cells * shard
    for ref in out_refs[1:]:
        ref[last : last + RIM_ROWS, :] = jnp.zeros((RIM_ROWS, rank), jnp.float32)
        for number, block in enumerate((conduct_ref[0], conduct_ref[1], baseline_ref[...])):
            start = number * 2 * TW
            ref[last : last + TH, start : start + TW] = block[:, :TW]
            ref[last : last + TH, start + TW : start + 2 * TW] = block[:, columns - TW :]


def gather_tiles(freq_count, where, ids, conduct, baseline, parts):
    pos_count = len(parts)
    cells, entries, rank = parts[0].shape
    tile_rows = pos_count
    shard = (TILE_DEV // freq_count + 1) * tile_rows
    return pl.pallas_call(
        functools.partial(gather_kernel, pos_count, freq_count, tile_rows, shard),
        in_specs=[pl.BlockSpec(memory_space=pltpu.SMEM)] + [pl.BlockSpec(memory_space=pltpu.VMEM)] * (3 + pos_count),
        out_specs=[pl.BlockSpec(memory_space=pltpu.VMEM)] * freq_count,
        out_shape=[jax.ShapeDtypeStruct((cells * shard, rank), jnp.float32)]
        + [jax.ShapeDtypeStruct((cells * shard + RIM_ROWS, rank), jnp.float32)] * (freq_count - 1),
        compiler_params=pltpu.CompilerParams(vmem_limit_bytes=VMEM_LIMIT),
        name="tiles",
    )(where, ids, conduct, baseline, *parts)


def energy_kernel(cells, shard, freq_count, where_ref, weights_ref, conduct_ref, baseline_ref, *refs):
    in_refs, out_ref = refs[:freq_count], refs[freq_count]
    rank = in_refs[0].shape[1]
    my_freq = where_ref[1]
    weights = jnp.broadcast_to(weights_ref[...], (8, rank))
    for cell in range(cells):
        span = slice(cell * shard, (cell + 1) * shard)
        summed = in_refs[0][span, :]
        for ref in in_refs[1:]:
            summed = summed + ref[span, :]
        energy = lax.dot_general(
            weights,
            summed * summed,
            (((1,), (1,)), ((), ())),
            precision=HIGHEST,
            preferred_element_type=jnp.float32,
        )
        out_ref[cell : cell + 1, 0:shard] = jnp.sqrt(energy[0:1] / rank + eps_value)
    last = cells * shard
    left = jnp.zeros((TH, LANES), jnp.float32)
    right = jnp.zeros((TH, LANES), jnp.float32)
    for distance in range(1, freq_count):
        edge = in_refs[distance][last : last + TH, 0:LANES]
        partner = my_freq ^ distance
        left = jnp.where(partner == my_freq - 1, edge, left)
        right = jnp.where(partner == my_freq + 1, edge, right)
    columns, width = baseline_ref.shape[1], out_ref.shape[1]
    for number, block in enumerate((conduct_ref[0], conduct_ref[1], baseline_ref[...])):
        span = slice(cells + number * TH, cells + (number + 1) * TH)
        start = number * 2 * TW
        out_ref[span, 0:columns] = block
        out_ref[span, columns : columns + TW] = right[:, start : start + TW]
        out_ref[span, LANES - TW : LANES] = left[:, start + TW : start + 2 * TW]


def energies(cells, shard, where, weights, conduct, baseline, shards):
    rows = cells + 3 * TH
    width = -(-max(shard, baseline.shape[1] + 2 * TW) // LANES) * LANES
    return pl.pallas_call(
        functools.partial(energy_kernel, cells, shard, len(shards)),
        in_specs=[pl.BlockSpec(memory_space=pltpu.SMEM)] + [pl.BlockSpec(memory_space=pltpu.VMEM)] * (3 + len(shards)),
        out_specs=pl.BlockSpec(memory_space=pltpu.VMEM),
        out_shape=jax.ShapeDtypeStruct((rows, width), jnp.float32),
        compiler_params=pltpu.CompilerParams(vmem_limit_bytes=VMEM_LIMIT),
        name="energies",
    )(where, weights, conduct, baseline, *shards)


def diffuse_kernel(cells, shard, where_ref, strips_ref, out_ref, field_ref):
    pos_count, _, width = strips_ref.shape
    tile_rows = pos_count
    tile_cols = shard // tile_rows
    groups = pos_count // TH
    my_pos = where_ref[0]
    tile_row = lax.broadcasted_iota(jnp.int32, (tile_rows, width), 0)
    spot = lax.broadcasted_iota(jnp.int32, (tile_rows, width), 1)
    here = (spot % tile_rows == tile_row) & (spot < shard)
    source = lax.broadcasted_iota(jnp.int32, (width, LANES), 0)
    target = lax.broadcasted_iota(jnp.int32, (width, LANES), 1)
    field = jnp.zeros((TH * tile_rows, LANES), jnp.float32)
    for group in range(groups):
        left = 1 if group * 2 >= groups else 0
        for cell in range(cells):
            col = (source // tile_rows - left) * TW + group * cells + cell
            place = ((target == (col + LANES) % LANES) & (source < shard)).astype(jnp.float32)
            spread = []
            for row in range(TH):
                line = strips_ref[row * groups + group, pl.ds(cell, 1), :]
                spread.append(jnp.where(here, jnp.broadcast_to(line, (tile_rows, width)), 0.0))
            field = field + jnp.dot(
                jnp.concatenate(spread, axis=0), place, precision=HIGHEST, preferred_element_type=jnp.float32
            )

    def strip(which, row):
        return strips_ref[:, cells + which * TH + row, 0:LANES]

    across_k = [strip(0, row) for row in range(TH)]
    along_k = [strip(1, row) for row in range(TH)]
    field = [field[row * tile_rows : (row + 1) * tile_rows] + strip(2, row) for row in range(TH)]

    def above(rows, row):
        if row:
            return rows[row - 1]
        return jnp.where(tile_row[:, :LANES] == 0, 0.0, pltpu.roll(rows[TH - 1], 1, 0))

    def below(rows, row):
        if row < TH - 1:
            return rows[row + 1]
        return jnp.where(tile_row[:, :LANES] == tile_rows - 1, 0.0, pltpu.roll(rows[0], tile_rows - 1, 0))

    north_k = [jnp.minimum(across_k[r], above(across_k, r)) for r in range(TH)]
    south_k = [jnp.minimum(across_k[r], below(across_k, r)) for r in range(TH)]
    west_k = [jnp.minimum(k, pltpu.roll(k, 1, 1)) for k in along_k]
    east_k = [jnp.minimum(k, pltpu.roll(k, LANES - 1, 1)) for k in along_k]
    for _ in range(PASSES):
        field = [
            field[r]
            + north_k[r] * (above(field, r) - field[r])
            + south_k[r] * (below(field, r) - field[r])
            + west_k[r] * (pltpu.roll(field[r], 1, 1) - field[r])
            + east_k[r] * (pltpu.roll(field[r], LANES - 1, 1) - field[r])
            for r in range(TH)
        ]
    for row in range(TH):
        field_ref[...] = field[row]
        out_ref[pl.ds(row, 1), :] = field_ref[pl.ds(my_pos, 1), 0 : out_ref.shape[1]]


def diffuse(cells, shard, where, strips, columns):
    return pl.pallas_call(
        functools.partial(diffuse_kernel, cells, shard),
        in_specs=[pl.BlockSpec(memory_space=pltpu.SMEM), pl.BlockSpec(memory_space=pltpu.VMEM)],
        out_specs=pl.BlockSpec(memory_space=pltpu.VMEM),
        out_shape=jax.ShapeDtypeStruct((TH, columns), jnp.float32),
        scratch_shapes=[pltpu.VMEM((strips.shape[0], LANES), jnp.float32)],
        compiler_params=pltpu.CompilerParams(vmem_limit_bytes=VMEM_LIMIT),
        name="diffuse",
    )(where, strips)


def swap(array, axis, distance):
    return lax.ppermute(array, axis, [(i, i ^ distance) for i in range(lax.axis_size(axis))])


def body(footprint, basis, weights, conduct, baseline):
    pos_local, freq_local, doubled, rank = basis.shape
    elements = doubled // 2
    foot = footprint.shape[1]
    pos_count = lax.axis_size("pos")
    freq_count = lax.axis_size("freq")
    columns = baseline.shape[1]
    sizes = (
        pos_count,
        freq_local * freq_count,
        pos_local * pos_count,
        elements,
        pos_local,
        freq_local,
        foot,
    )
    where = jnp.stack([lax.axis_index("pos"), lax.axis_index("freq")]).astype(jnp.int32)
    ids = footprint.reshape(pos_count, pos_local * foot)
    split = basis.reshape(pos_local, freq_local, 2, elements, rank)
    groups = pos_count // TH
    half = groups // 2
    parts = [None] * pos_count
    rounds = (
        tuple(range(3 * groups, 4 * groups)),
        tuple(range(2 * groups, 2 * groups + half)) + tuple(range(groups, groups + half)),
        tuple(range(2 * groups + half, 3 * groups)) + tuple(range(groups + half, 2 * groups)),
        tuple(range(groups)),
    )
    operands, after = (where, footprint, split), ()
    for turn, distances in enumerate(rounds):
        sent = project(sizes, rounds, turn, operands, after)
        for number, distance in enumerate(distances):
            parts[distance] = swap(sent[number], "pos", distance) if distance else sent[number]
        if turn == 0:
            operands = (where,) + tuple(sent[groups:])
        after = (sent[0],)
        if turn == 2:
            after += tuple(parts[distance] for past in rounds[:2] for distance in past)
    cells, shard = CELLS // pos_count, (TILE_DEV // freq_count + 1) * pos_count
    tiles = gather_tiles(freq_count, where, ids, conduct, baseline, parts)
    shards = [swap(tiles[d], "freq", d) if d else tiles[d] for d in range(freq_count)]
    strip = energies(cells, shard, where, weights.reshape(1, rank), conduct, baseline, shards)
    strips = lax.all_gather(strip, "pos")
    return diffuse(cells, shard, where, strips, columns)


def solution(mesh):
    return jax.shard_map(
        body,
        mesh=mesh,
        in_specs=(P(), P("pos", "freq", None, None), P(), P(None, "pos", "freq"), P("pos", "freq")),
        out_specs=P("pos", "freq"),
        check_vma=False,
    )
```

```python
import functools
import math

import jax
import jax.numpy as jnp
from jax import lax
from jax.experimental import pallas as pl
from jax.experimental.pallas import tpu as pltpu
from jax.sharding import PartitionSpec as P

TH = 4
TW = 8
CELLS = TH * TW
TILE_DEV = 32
PASSES = 3
LANES = 128
RIM_ROWS = 8
ELEM_BLOCK = 256
AHEAD = 3

elem_pitch = 0.125
cell_spacing = 0.7
top_depth = 4.0
eps_value = 1e-06

SIN_PI = tuple(
    math.sqrt(2.0) * (1.0 - 2e-6) * term
    for term in (3.1415903568267822, -5.1674065589904785, 2.5440104007720947, -0.5594624280929565)
)

HIGHEST = lax.Precision.HIGHEST
VMEM_LIMIT = 24 * 1024 * 1024
VMEM_LIMIT_FIRST = 42 * 1024 * 1024


def half_turn(turns):
    x = turns - jnp.round(turns)
    square = x * x
    s = SIN_PI[-1]
    for term in SIN_PI[-2::-1]:
        s = s * square + term
    s = s * x
    rest = 2.0 - s * s
    return rest * lax.rsqrt(rest), s, rest - 1.0


def waves(distance, first_turns, step_turns, count):
    c, s, cosine = half_turn(first_turns * distance)
    amplitude = lax.rsqrt(distance)
    last = amplitude * cosine, (amplitude * c) * s
    c, s, cosine = half_turn(step_turns * distance)
    sine = c * s
    now = last[0] * cosine - last[1] * sine, last[1] * cosine + last[0] * sine
    found = [last, now]
    twice = cosine + cosine
    for _ in range(count - 2):
        now, last = tuple(twice * a - b for a, b in zip(now, last)), now
        found.append(now)
    return found[:count]


def project_kernel(sizes, rounds, turn, waits, *refs):
    first = turn == 0
    pos_count, freqs, positions, elements, pos_local, freq_local, foot = sizes
    groups = pos_count // TH
    per_dest = TW // groups
    blocks = elements // ELEM_BLOCK
    steps = pos_local * blocks
    where_ref, refs = refs[0], refs[1:]
    if first:
        (foot_ref, basis_ref), refs = refs[:2], refs[2:]
        out_refs, refs = refs[:groups], refs[groups:]
        kept_ref, depth_ref, lateral_ref, element_ref, green_even, green_odd, total_ref, held_ref, sems, kept_sems = refs
    else:
        held_ref, depth_ref, lateral_ref, element_ref = refs[:4]
        out_refs, refs = refs[4 + waits : 4 + waits + groups], refs[4 + waits + groups :]
        green_even, green_odd, total_ref = refs
    my_pos, my_freq = where_ref[0], where_ref[1]

    def fetch(step):
        offset, block = step // blocks, step % blocks
        spot = pl.ds(block * ELEM_BLOCK, ELEM_BLOCK)
        return pltpu.make_async_copy(basis_ref.at[offset, :, :, spot, :], held_ref.at[step], sems.at[step])

    def keep(step):
        return pltpu.make_async_copy(held_ref.at[step], kept_ref.at[step], kept_sems.at[step])

    if first:
        for step in range(AHEAD):
            fetch(step).start()

    first_freq = (my_freq * freq_local).astype(jnp.float32)
    first_turns = top_depth * (0.5 + first_freq / freqs)
    step_turns = top_depth / freqs

    if first:
        scale = 1.0 / top_depth
        row = lax.broadcasted_iota(jnp.int32, (TW, LANES), 0)
        lane = lax.broadcasted_iota(jnp.int32, (TW, LANES), 1)
        places = []
        for distances in rounds:
            target = my_pos ^ functools.reduce(
                lambda rest, here: jnp.where(row // per_dest == here, distances[here], rest), range(1, groups), distances[0]
            )
            places.append((target // groups, (target % groups) * per_dest + row % per_dest))
        for offset in range(pos_local):
            pos_global = my_pos * pos_local + offset
            centre = pos_global.astype(jnp.float32) * (cell_spacing * TW * TILE_DEV / positions)
            for piece in range(elements // LANES):
                index = (piece * LANES + lane).astype(jnp.float32)
                element_ref[offset, piece] = scale * ((index - 0.5 * (elements - 1)) * elem_pitch + centre)

            def place(entry, _, offset=offset, pos_global=pos_global):
                tile = foot_ref[pos_global, entry]
                for number, (cell_row, cell_col) in enumerate(places):
                    grid_row = ((tile // TILE_DEV) * TH + cell_row).astype(jnp.float32)
                    grid_col = ((tile % TILE_DEV) * TW + cell_col).astype(jnp.float32)
                    depth = scale * (top_depth + cell_spacing * grid_row)
                    depth_ref[number, offset, entry] = depth * depth
                    lateral_ref[number, offset, entry] = scale * (cell_spacing * grid_col)
                return 0

            lax.fori_loop(0, foot, place, 0, unroll=4)
    total_ref[...] = jnp.zeros_like(total_ref)

    def green(step, green_ref):
        offset, block = step // blocks, step % blocks
        for pair in range(foot // 2):
            entry = 2 * pair
            depth_square = depth_ref[turn, offset, pl.ds(entry, 2)].reshape(2 * TW, LANES)
            lateral = lateral_ref[turn, offset, pl.ds(entry, 2)].reshape(2 * TW, LANES)
            spot = pl.ds(entry * TW, 2 * TW)
            for sub in range(ELEM_BLOCK // LANES):
                element = element_ref[offset, block * (ELEM_BLOCK // LANES) + sub]
                across = lateral - jnp.concatenate([element, element], axis=0)
                square = depth_square + across * across
                distance = square * lax.rsqrt(square)
                for number, both in enumerate(waves(distance, first_turns, step_turns, freq_local)):
                    for part_of, wave in enumerate(both):
                        start = (number * 2 + part_of) * ELEM_BLOCK + sub * LANES
                        green_ref[spot, start : start + LANES] = wave.astype(jnp.bfloat16)

    def apply(step, green_ref):
        offset = step // blocks
        weights = held_ref[step].reshape(freq_local * 2 * ELEM_BLOCK, -1)
        gain = jnp.dot(green_ref[...], weights, preferred_element_type=jnp.float32)
        for half in range(gain.shape[1] // LANES):
            total_ref[offset, half] = total_ref[offset, half] + gain[:, half * LANES : (half + 1) * LANES]

    def run(make, into, use, out_of):
        if use is not None:
            if first:
                fetch(use).wait()
                keep(use).start()
                if isinstance(use, int):
                    if use + AHEAD < steps:
                        fetch(use + AHEAD).start()
                else:
                    pl.when(use + AHEAD < steps)(lambda: fetch(use + AHEAD).start())
            apply(use, out_of)
        if make is not None:
            green(make, into)

    run(0, green_even, None, None)

    def two(pair, _):
        run(2 * pair + 1, green_odd, 2 * pair, green_even)
        run(2 * pair + 2, green_even, 2 * pair + 1, green_odd)
        return 0

    lax.fori_loop(0, steps // 2 - 1, two, 0)
    run(steps - 1, green_odd, steps - 2, green_even)
    run(None, None, steps - 1, green_odd)

    if first:
        for step in range(steps):
            keep(step).wait()
    for offset in range(pos_local):
        for group in range(groups):
            for cell in range(per_dest):
                for half in range(total_ref.shape[1]):
                    out_refs[group][cell, offset * foot : (offset + 1) * foot, half * LANES : (half + 1) * LANES] = (
                        total_ref[offset, half, pl.ds(group * per_dest + cell, foot, stride=TW), :]
                    )


def project(sizes, rounds, turn, operands, after):
    first = turn == 0
    pos_count, freqs, positions, elements, pos_local, freq_local, foot = sizes
    groups = pos_count // TH
    per_dest = TW // groups
    basis = operands[2] if first else operands[1]
    rank = basis.shape[-1]
    rows = foot * TW
    steps = pos_local * elements // ELEM_BLOCK
    flops = 2 * pos_local * rows * freq_local * 2 * elements * rank

    def shape(*dims, dtype=jnp.float32):
        return jax.ShapeDtypeStruct(dims, dtype)

    vmem, smem = pl.BlockSpec(memory_space=pltpu.VMEM), pl.BlockSpec(memory_space=pltpu.SMEM)
    out_shape = [shape(per_dest, pos_local * foot, rank)] * groups
    if first:
        in_specs = [smem, smem, pl.BlockSpec(memory_space=pl.ANY)]
        out_shape += [
            shape(steps, freq_local, 2, ELEM_BLOCK, rank, dtype=jnp.bfloat16),
            shape(len(rounds), pos_local, foot, TW, LANES),
            shape(len(rounds), pos_local, foot, TW, LANES),
            shape(pos_local, elements // LANES, TW, LANES),
        ]
    else:
        in_specs = [smem] + [vmem] * 4 + [pl.BlockSpec(memory_space=pl.ANY)] * len(after)
    green = pltpu.VMEM((rows, freq_local * 2 * ELEM_BLOCK), jnp.bfloat16)
    return pl.pallas_call(
        functools.partial(project_kernel, sizes, rounds, turn, len(after)),
        in_specs=in_specs,
        out_specs=[vmem] * groups
        + ([pl.BlockSpec(memory_space=pl.ANY)] + [vmem] * 3 if first else []),
        out_shape=out_shape,
        scratch_shapes=[green, green, pltpu.VMEM((pos_local, rank // LANES, rows, LANES), jnp.float32)]
        + (
            [
                pltpu.VMEM((steps, freq_local, 2, ELEM_BLOCK, rank), jnp.bfloat16),
                pltpu.SemaphoreType.DMA((steps,)),
                pltpu.SemaphoreType.DMA((steps,)),
            ]
            if first
            else []
        ),
        compiler_params=pltpu.CompilerParams(vmem_limit_bytes=VMEM_LIMIT_FIRST if first else VMEM_LIMIT),
        cost_estimate=pl.CostEstimate(flops=flops, bytes_accessed=flops, transcendentals=0),
        name=f"project_{turn}",
    )(*operands, *after)


def two_terms(values):
    high = values.astype(jnp.bfloat16)
    return high, (values - high.astype(jnp.float32)).astype(jnp.bfloat16)


def rim_spot(last, number):
    start = last + number % 2 * TH
    return slice(start, start + TH), number // 2 * LANES


def gather_kernel(pos_count, freq_count, tile_rows, shard, where_ref, ids_ref, conduct_ref, baseline_ref, *refs):
    in_refs, out_refs = refs[:pos_count], refs[pos_count:]
    cells, entries, rank = in_refs[0].shape
    columns = baseline_ref.shape[1]
    tile_cols = shard // tile_rows
    groups = pos_count // TH
    my_pos, my_freq = where_ref[0], where_ref[1]
    left = (lax.rem(my_pos, groups) * 2 >= groups).astype(jnp.int32)
    row = lax.broadcasted_iota(jnp.int32, (shard, entries), 0)
    wanted = (row % tile_rows) * TILE_DEV + row // tile_rows - left
    hot = []
    for other in range(freq_count):
        base = (my_freq ^ other) * (tile_cols - 1)
        col = row // tile_rows - left + base
        hot_row = []
        for source in range(pos_count):
            ids = ids_ref[pl.ds(my_pos ^ source, 1), :]
            hit = (wanted + base == ids) & (col >= 0) & (col < TILE_DEV)
            hot_row.append(hit.astype(jnp.float32).astype(jnp.bfloat16))
        hot_row = jnp.concatenate(hot_row, axis=1)
        hot.append(jnp.concatenate([hot_row] * 2, axis=1))
    for cell in range(cells):
        values = jnp.concatenate([ref[cell] for ref in in_refs], axis=0)
        terms = jnp.concatenate(two_terms(values), axis=0)
        for other in range(freq_count):
            span = slice(cell * shard, (cell + 1) * shard)
            out_refs[other][span, :] = jnp.dot(hot[other], terms, preferred_element_type=jnp.float32)
    last = cells * shard
    for ref in out_refs[1:]:
        for number, block in enumerate((conduct_ref[0], conduct_ref[1], baseline_ref[...])):
            rows, lane = rim_spot(last, number)
            ref[rows, lane + columns : lane + columns + TW] = block[:, :TW]
            ref[rows, lane + LANES - TW : lane + LANES] = block[:, columns - TW :]


def gather_tiles(freq_count, where, ids, conduct, baseline, parts):
    pos_count = len(parts)
    cells, entries, rank = parts[0].shape
    tile_rows = pos_count
    shard = (TILE_DEV // freq_count + 1) * tile_rows
    return pl.pallas_call(
        functools.partial(gather_kernel, pos_count, freq_count, tile_rows, shard),
        in_specs=[pl.BlockSpec(memory_space=pltpu.SMEM)] + [pl.BlockSpec(memory_space=pltpu.VMEM)] * (3 + pos_count),
        out_specs=[pl.BlockSpec(memory_space=pltpu.VMEM)] * freq_count,
        out_shape=[jax.ShapeDtypeStruct((cells * shard, rank), jnp.float32)]
        + [jax.ShapeDtypeStruct((cells * shard + RIM_ROWS, rank), jnp.float32)] * (freq_count - 1),
        compiler_params=pltpu.CompilerParams(vmem_limit_bytes=VMEM_LIMIT),
        name="tiles",
    )(where, ids, conduct, baseline, *parts)


def energy_kernel(cells, shard, freq_count, where_ref, weights_ref, conduct_ref, baseline_ref, *refs):
    in_refs, out_ref = refs[:freq_count], refs[freq_count]
    rank = in_refs[0].shape[1]
    my_freq = where_ref[1]
    weights = jnp.broadcast_to(weights_ref[...], (8, rank))
    for cell in range(cells):
        span = slice(cell * shard, (cell + 1) * shard)
        summed = in_refs[0][span, :]
        for ref in in_refs[1:]:
            summed = summed + ref[span, :]
        energy = lax.dot_general(
            weights,
            summed * summed,
            (((1,), (1,)), ((), ())),
            precision=HIGHEST,
            preferred_element_type=jnp.float32,
        )
        out_ref[cell : cell + 1, 0:shard] = jnp.sqrt(energy[0:1] / rank + eps_value)
    last = cells * shard
    columns = baseline_ref.shape[1]
    for number, block in enumerate((conduct_ref[0], conduct_ref[1], baseline_ref[...])):
        rows, lane = rim_spot(last, number)
        left = jnp.zeros((TH, LANES), jnp.float32)
        right = jnp.zeros((TH, LANES), jnp.float32)
        for distance in range(1, freq_count):
            edge = in_refs[distance][rows, lane : lane + LANES]
            partner = my_freq ^ distance
            left = jnp.where(partner == my_freq - 1, edge, left)
            right = jnp.where(partner == my_freq + 1, edge, right)
        span = slice(cells + number * TH, cells + (number + 1) * TH)
        out_ref[span, 0:columns] = block
        out_ref[span, columns : columns + TW] = right[:, columns : columns + TW]
        out_ref[span, LANES - TW : LANES] = left[:, LANES - TW :]


def energies(cells, shard, where, weights, conduct, baseline, shards):
    rows = cells + 3 * TH
    width = -(-max(shard, baseline.shape[1] + 2 * TW) // LANES) * LANES
    return pl.pallas_call(
        functools.partial(energy_kernel, cells, shard, len(shards)),
        in_specs=[pl.BlockSpec(memory_space=pltpu.SMEM)] + [pl.BlockSpec(memory_space=pltpu.VMEM)] * (3 + len(shards)),
        out_specs=pl.BlockSpec(memory_space=pltpu.VMEM),
        out_shape=jax.ShapeDtypeStruct((rows, width), jnp.float32),
        compiler_params=pltpu.CompilerParams(vmem_limit_bytes=VMEM_LIMIT),
        name="energies",
    )(where, weights, conduct, baseline, *shards)


def diffuse_kernel(cells, shard, where_ref, strips_ref, out_ref, field_ref):
    pos_count, _, width = strips_ref.shape
    tile_rows = pos_count
    tile_cols = shard // tile_rows
    groups = pos_count // TH
    my_pos = where_ref[0]
    tile_row = lax.broadcasted_iota(jnp.int32, (tile_rows, width), 0)
    spot = lax.broadcasted_iota(jnp.int32, (tile_rows, width), 1)
    here = (spot % tile_rows == tile_row) & (spot < shard)
    source = lax.broadcasted_iota(jnp.int32, (width, LANES), 0)
    target = lax.broadcasted_iota(jnp.int32, (width, LANES), 1)
    field = jnp.zeros((TH * tile_rows, LANES), jnp.float32)
    for group in range(groups):
        left = 1 if group * 2 >= groups else 0
        for cell in range(cells):
            col = (source // tile_rows - left) * TW + group * cells + cell
            place = ((target == (col + LANES) % LANES) & (source < shard)).astype(jnp.float32)
            spread = []
            for row in range(TH):
                line = strips_ref[row * groups + group, pl.ds(cell, 1), :]
                spread.append(jnp.where(here, jnp.broadcast_to(line, (tile_rows, width)), 0.0))
            field = field + jnp.dot(
                jnp.concatenate(spread, axis=0), place, precision=HIGHEST, preferred_element_type=jnp.float32
            )

    def strip(which, row):
        return strips_ref[:, cells + which * TH + row, 0:LANES]

    across_k = [strip(0, row) for row in range(TH)]
    along_k = [strip(1, row) for row in range(TH)]
    field = [field[row * tile_rows : (row + 1) * tile_rows] + strip(2, row) for row in range(TH)]

    def above(rows, row):
        if row:
            return rows[row - 1]
        return jnp.where(tile_row[:, :LANES] == 0, 0.0, pltpu.roll(rows[TH - 1], 1, 0))

    def below(rows, row):
        if row < TH - 1:
            return rows[row + 1]
        return jnp.where(tile_row[:, :LANES] == tile_rows - 1, 0.0, pltpu.roll(rows[0], tile_rows - 1, 0))

    north_k = [jnp.minimum(across_k[r], above(across_k, r)) for r in range(TH)]
    south_k = [jnp.minimum(across_k[r], below(across_k, r)) for r in range(TH)]
    west_k = [jnp.minimum(k, pltpu.roll(k, 1, 1)) for k in along_k]
    east_k = [jnp.minimum(k, pltpu.roll(k, LANES - 1, 1)) for k in along_k]
    for _ in range(PASSES):
        field = [
            field[r]
            + north_k[r] * (above(field, r) - field[r])
            + south_k[r] * (below(field, r) - field[r])
            + west_k[r] * (pltpu.roll(field[r], 1, 1) - field[r])
            + east_k[r] * (pltpu.roll(field[r], LANES - 1, 1) - field[r])
            for r in range(TH)
        ]
    for row in range(TH):
        field_ref[...] = field[row]
        out_ref[pl.ds(row, 1), :] = field_ref[pl.ds(my_pos, 1), 0 : out_ref.shape[1]]


def diffuse(cells, shard, where, strips, columns):
    return pl.pallas_call(
        functools.partial(diffuse_kernel, cells, shard),
        in_specs=[pl.BlockSpec(memory_space=pltpu.SMEM), pl.BlockSpec(memory_space=pltpu.VMEM)],
        out_specs=pl.BlockSpec(memory_space=pltpu.VMEM),
        out_shape=jax.ShapeDtypeStruct((TH, columns), jnp.float32),
        scratch_shapes=[pltpu.VMEM((strips.shape[0], LANES), jnp.float32)],
        compiler_params=pltpu.CompilerParams(vmem_limit_bytes=VMEM_LIMIT),
        name="diffuse",
    )(where, strips)


def swap(array, axis, distance):
    return lax.ppermute(array, axis, [(i, i ^ distance) for i in range(lax.axis_size(axis))])


def body(footprint, basis, weights, conduct, baseline):
    pos_local, freq_local, doubled, rank = basis.shape
    elements = doubled // 2
    foot = footprint.shape[1]
    pos_count = lax.axis_size("pos")
    freq_count = lax.axis_size("freq")
    columns = baseline.shape[1]
    sizes = (
        pos_count,
        freq_local * freq_count,
        pos_local * pos_count,
        elements,
        pos_local,
        freq_local,
        foot,
    )
    where = jnp.stack([lax.axis_index("pos"), lax.axis_index("freq")]).astype(jnp.int32)
    ids = footprint.reshape(pos_count, pos_local * foot)
    split = basis.reshape(pos_local, freq_local, 2, elements, rank)
    groups = pos_count // TH
    half = groups // 2
    parts = [None] * pos_count
    rounds = (
        tuple(range(3 * groups, 4 * groups)),
        tuple(range(2 * groups, 2 * groups + half)) + tuple(range(groups, groups + half)),
        tuple(range(2 * groups + half, 3 * groups)) + tuple(range(groups + half, 2 * groups)),
        tuple(range(groups)),
    )
    operands, after = (where, footprint, split), ()
    for turn, distances in enumerate(rounds):
        sent = project(sizes, rounds, turn, operands, after)
        for number, distance in enumerate(distances):
            parts[distance] = swap(sent[number], "pos", distance) if distance else sent[number]
        if turn == 0:
            operands = (where,) + tuple(sent[groups:])
        after = (sent[0],)
        if turn == 2:
            after += tuple(parts[-groups:])
    cells, shard = CELLS // pos_count, (TILE_DEV // freq_count + 1) * pos_count
    tiles = gather_tiles(freq_count, where, ids, conduct, baseline, parts)
    shards = [swap(tiles[d], "freq", d) if d else tiles[d] for d in range(freq_count)]
    strip = energies(cells, shard, where, weights.reshape(1, rank), conduct, baseline, shards)
    strips = lax.all_gather(strip, "pos")
    return diffuse(cells, shard, where, strips, columns)


def solution(mesh):
    return jax.shard_map(
        body,
        mesh=mesh,
        in_specs=(P(), P("pos", "freq", None, None), P(), P(None, "pos", "freq"), P("pos", "freq")),
        out_specs=P("pos", "freq"),
        check_vma=False,
    )
```

```python
import functools
import math

import jax
import jax.numpy as jnp
from jax import lax
from jax.experimental import pallas as pl
from jax.experimental.pallas import tpu as pltpu
from jax.sharding import PartitionSpec as P

TH = 4
TW = 8
CELLS = TH * TW
TILE_DEV = 32
PASSES = 3
LANES = 128
RIM_ROWS = 8
ELEM_BLOCK = 256
AHEAD = 3

elem_pitch = 0.125
cell_spacing = 0.7
top_depth = 4.0
eps_value = 1e-06

SIN_PI = tuple(
    math.sqrt(2.0) * (1.0 - 2e-6) * term
    for term in (3.1415903568267822, -5.1674065589904785, 2.5440104007720947, -0.5594624280929565)
)

HIGHEST = lax.Precision.HIGHEST
VMEM_LIMIT = 24 * 1024 * 1024
VMEM_LIMIT_FIRST = 42 * 1024 * 1024


def half_turn(turns):
    x = turns - jnp.round(turns)
    square = x * x
    s = SIN_PI[-1]
    for term in SIN_PI[-2::-1]:
        s = s * square + term
    s = s * x
    rest = 2.0 - s * s
    return rest * lax.rsqrt(rest), s, rest - 1.0


def waves(distance, first_turns, step_turns, count):
    c, s, cosine = half_turn(first_turns * distance)
    amplitude = lax.rsqrt(distance)
    last = amplitude * cosine, (amplitude * c) * s
    c, s, cosine = half_turn(step_turns * distance)
    sine = c * s
    now = last[0] * cosine - last[1] * sine, last[1] * cosine + last[0] * sine
    found = [last, now]
    twice = cosine + cosine
    for _ in range(count - 2):
        now, last = tuple(twice * a - b for a, b in zip(now, last)), now
        found.append(now)
    return found[:count]


def project_kernel(sizes, rounds, turn, waits, *refs):
    first = turn == 0
    pos_count, freqs, positions, elements, pos_local, freq_local, foot = sizes
    groups = pos_count // TH
    per_dest = TW // groups
    blocks = elements // ELEM_BLOCK
    steps = pos_local * blocks
    if first:
        (foot_ref, basis_ref), refs = refs[:2], refs[2:]
        out_refs, refs = refs[:groups], refs[groups:]
        held_ref, depth_ref, lateral_ref, element_ref, green_even, green_odd, total_ref, sems = refs
    else:
        held_ref, depth_ref, lateral_ref, element_ref = refs[:4]
        out_refs, refs = refs[4 + waits : 4 + waits + groups], refs[4 + waits + groups :]
        green_even, green_odd, total_ref = refs
    my_pos, my_freq = lax.axis_index("pos"), lax.axis_index("freq")

    def fetch(step):
        offset, block = step // blocks, step % blocks
        spot = pl.ds(block * ELEM_BLOCK, ELEM_BLOCK)
        return pltpu.make_async_copy(basis_ref.at[offset, :, :, spot, :], held_ref.at[step], sems.at[step])

    if first:
        for step in range(AHEAD):
            fetch(step).start()

    first_freq = (my_freq * freq_local).astype(jnp.float32)
    first_turns = top_depth * (0.5 + first_freq / freqs)
    step_turns = top_depth / freqs

    if first:
        scale = 1.0 / top_depth
        row = lax.broadcasted_iota(jnp.int32, (TW, LANES), 0)
        lane = lax.broadcasted_iota(jnp.int32, (TW, LANES), 1)
        places = []
        for distances in rounds:
            target = my_pos ^ functools.reduce(
                lambda rest, here: jnp.where(row // per_dest == here, distances[here], rest), range(1, groups), distances[0]
            )
            places.append((target // groups, (target % groups) * per_dest + row % per_dest))
        for offset in range(pos_local):
            pos_global = my_pos * pos_local + offset
            centre = pos_global.astype(jnp.float32) * (cell_spacing * TW * TILE_DEV / positions)
            for piece in range(elements // LANES):
                index = (piece * LANES + lane).astype(jnp.float32)
                element_ref[offset, piece] = scale * ((index - 0.5 * (elements - 1)) * elem_pitch + centre)

            def place(entry, _, offset=offset, pos_global=pos_global):
                tile = foot_ref[pos_global, entry]
                for number, (cell_row, cell_col) in enumerate(places):
                    grid_row = ((tile // TILE_DEV) * TH + cell_row).astype(jnp.float32)
                    grid_col = ((tile % TILE_DEV) * TW + cell_col).astype(jnp.float32)
                    depth = scale * (top_depth + cell_spacing * grid_row)
                    depth_ref[number, offset, entry] = depth * depth
                    lateral_ref[number, offset, entry] = scale * (cell_spacing * grid_col)
                return 0

            lax.fori_loop(0, foot, place, 0, unroll=4)
    total_ref[...] = jnp.zeros_like(total_ref)

    def green(step, green_ref):
        offset, block = step // blocks, step % blocks
        for pair in range(foot // 2):
            entry = 2 * pair
            depth_square = depth_ref[turn, offset, pl.ds(entry, 2)].reshape(2 * TW, LANES)
            lateral = lateral_ref[turn, offset, pl.ds(entry, 2)].reshape(2 * TW, LANES)
            spot = pl.ds(entry * TW, 2 * TW)
            for sub in range(ELEM_BLOCK // LANES):
                element = element_ref[offset, block * (ELEM_BLOCK // LANES) + sub]
                across = lateral - jnp.concatenate([element, element], axis=0)
                square = depth_square + across * across
                distance = square * lax.rsqrt(square)
                for number, both in enumerate(waves(distance, first_turns, step_turns, freq_local)):
                    for part_of, wave in enumerate(both):
                        start = (number * 2 + part_of) * ELEM_BLOCK + sub * LANES
                        green_ref[spot, start : start + LANES] = wave.astype(jnp.bfloat16)

    def apply(step, green_ref):
        offset = step // blocks
        weights = held_ref[step].reshape(freq_local * 2 * ELEM_BLOCK, -1)
        gain = jnp.dot(green_ref[...], weights, preferred_element_type=jnp.float32)
        for half in range(gain.shape[1] // LANES):
            total_ref[offset, half] = total_ref[offset, half] + gain[:, half * LANES : (half + 1) * LANES]

    def run(make, into, use, out_of):
        if use is not None:
            if first:
                fetch(use).wait()
                if isinstance(use, int):
                    if use + AHEAD < steps:
                        fetch(use + AHEAD).start()
                else:
                    pl.when(use + AHEAD < steps)(lambda: fetch(use + AHEAD).start())
            apply(use, out_of)
        if make is not None:
            green(make, into)

    run(0, green_even, None, None)

    def two(pair, _):
        run(2 * pair + 1, green_odd, 2 * pair, green_even)
        run(2 * pair + 2, green_even, 2 * pair + 1, green_odd)
        return 0

    lax.fori_loop(0, steps // 2 - 1, two, 0)
    run(steps - 1, green_odd, steps - 2, green_even)
    run(None, None, steps - 1, green_odd)

    for offset in range(pos_local):
        for group in range(groups):
            for cell in range(per_dest):
                for half in range(total_ref.shape[1]):
                    out_refs[group][cell, offset * foot : (offset + 1) * foot, half * LANES : (half + 1) * LANES] = (
                        total_ref[offset, half, pl.ds(group * per_dest + cell, foot, stride=TW), :]
                    )


def project(sizes, rounds, turn, operands, after):
    first = turn == 0
    pos_count, freqs, positions, elements, pos_local, freq_local, foot = sizes
    groups = pos_count // TH
    per_dest = TW // groups
    basis = operands[1] if first else operands[0]
    rank = basis.shape[-1]
    rows = foot * TW
    steps = pos_local * elements // ELEM_BLOCK
    flops = 2 * pos_local * rows * freq_local * 2 * elements * rank

    def shape(*dims, dtype=jnp.float32):
        return jax.ShapeDtypeStruct(dims, dtype)

    vmem, smem = pl.BlockSpec(memory_space=pltpu.VMEM), pl.BlockSpec(memory_space=pltpu.SMEM)
    out_shape = [shape(per_dest, pos_local * foot, rank)] * groups
    if first:
        in_specs = [smem, pl.BlockSpec(memory_space=pl.ANY)]
        out_shape += [
            shape(steps, freq_local, 2, ELEM_BLOCK, rank, dtype=jnp.bfloat16),
            shape(len(rounds), pos_local, foot, TW, LANES),
            shape(len(rounds), pos_local, foot, TW, LANES),
            shape(pos_local, elements // LANES, TW, LANES),
        ]
    else:
        in_specs = [vmem] * 4 + [pl.BlockSpec(memory_space=pl.ANY)] * len(after)
    green = pltpu.VMEM((rows, freq_local * 2 * ELEM_BLOCK), jnp.bfloat16)
    return pl.pallas_call(
        functools.partial(project_kernel, sizes, rounds, turn, len(after)),
        in_specs=in_specs,
        out_specs=[vmem] * len(out_shape),
        out_shape=out_shape,
        scratch_shapes=[green, green, pltpu.VMEM((pos_local, rank // LANES, rows, LANES), jnp.float32)]
        + ([pltpu.SemaphoreType.DMA((steps,))] if first else []),
        compiler_params=pltpu.CompilerParams(vmem_limit_bytes=VMEM_LIMIT_FIRST if first else VMEM_LIMIT),
        cost_estimate=pl.CostEstimate(flops=flops, bytes_accessed=flops, transcendentals=0),
        name=f"project_{turn}",
    )(*operands, *after)


def two_terms(values):
    high = values.astype(jnp.bfloat16)
    return high, (values - high.astype(jnp.float32)).astype(jnp.bfloat16)


def rim_spot(last, number):
    start = last + number % 2 * TH
    return slice(start, start + TH), number // 2 * LANES


def gather_kernel(pos_count, freq_count, tile_rows, shard, ids_ref, conduct_ref, baseline_ref, *refs):
    in_refs, out_refs = refs[:pos_count], refs[pos_count:]
    cells, entries, rank = in_refs[0].shape
    columns = baseline_ref.shape[1]
    tile_cols = shard // tile_rows
    groups = pos_count // TH
    my_pos, my_freq = lax.axis_index("pos"), lax.axis_index("freq")
    left = (lax.rem(my_pos, groups) * 2 >= groups).astype(jnp.int32)
    row = lax.broadcasted_iota(jnp.int32, (shard, entries), 0)
    wanted = (row % tile_rows) * TILE_DEV + row // tile_rows - left
    hot = []
    for other in range(freq_count):
        base = (my_freq ^ other) * (tile_cols - 1)
        col = row // tile_rows - left + base
        hot_row = []
        for source in range(pos_count):
            ids = ids_ref[pl.ds(my_pos ^ source, 1), :]
            hit = (wanted + base == ids) & (col >= 0) & (col < TILE_DEV)
            hot_row.append(hit.astype(jnp.float32).astype(jnp.bfloat16))
        hot_row = jnp.concatenate(hot_row, axis=1)
        hot.append(jnp.concatenate([hot_row] * 2, axis=1))
    for cell in range(cells):
        values = jnp.concatenate([ref[cell] for ref in in_refs], axis=0)
        terms = jnp.concatenate(two_terms(values), axis=0)
        for other in range(freq_count):
            span = slice(cell * shard, (cell + 1) * shard)
            out_refs[other][span, :] = jnp.dot(hot[other], terms, preferred_element_type=jnp.float32)
    last = cells * shard
    for ref in out_refs[1:]:
        for number, block in enumerate((conduct_ref[0], conduct_ref[1], baseline_ref[...])):
            rows, lane = rim_spot(last, number)
            ref[rows, lane + columns : lane + columns + TW] = block[:, :TW]
            ref[rows, lane + LANES - TW : lane + LANES] = block[:, columns - TW :]


def gather_tiles(freq_count, ids, conduct, baseline, parts):
    pos_count = len(parts)
    cells, entries, rank = parts[0].shape
    tile_rows = pos_count
    shard = (TILE_DEV // freq_count + 1) * tile_rows
    return pl.pallas_call(
        functools.partial(gather_kernel, pos_count, freq_count, tile_rows, shard),
        in_specs=[pl.BlockSpec(memory_space=pltpu.VMEM)] * (3 + pos_count),
        out_specs=[pl.BlockSpec(memory_space=pltpu.VMEM)] * freq_count,
        out_shape=[jax.ShapeDtypeStruct((cells * shard, rank), jnp.float32)]
        + [jax.ShapeDtypeStruct((cells * shard + RIM_ROWS, rank), jnp.float32)] * (freq_count - 1),
        compiler_params=pltpu.CompilerParams(vmem_limit_bytes=VMEM_LIMIT),
        name="tiles",
    )(ids, conduct, baseline, *parts)


def energy_kernel(cells, shard, freq_count, weights_ref, conduct_ref, baseline_ref, *refs):
    in_refs, out_ref = refs[:freq_count], refs[freq_count]
    rank = in_refs[0].shape[1]
    my_freq = lax.axis_index("freq")
    weights = jnp.broadcast_to(weights_ref[...], (8, rank))
    for cell in range(cells):
        span = slice(cell * shard, (cell + 1) * shard)
        summed = in_refs[0][span, :]
        for ref in in_refs[1:]:
            summed = summed + ref[span, :]
        energy = lax.dot_general(
            weights,
            summed * summed,
            (((1,), (1,)), ((), ())),
            precision=HIGHEST,
            preferred_element_type=jnp.float32,
        )
        out_ref[cell : cell + 1, 0:shard] = jnp.sqrt(energy[0:1] / rank + eps_value)
    last = cells * shard
    columns = baseline_ref.shape[1]
    for number, block in enumerate((conduct_ref[0], conduct_ref[1], baseline_ref[...])):
        rows, lane = rim_spot(last, number)
        left = jnp.zeros((TH, LANES), jnp.float32)
        right = jnp.zeros((TH, LANES), jnp.float32)
        for distance in range(1, freq_count):
            edge = in_refs[distance][rows, lane : lane + LANES]
            partner = my_freq ^ distance
            left = jnp.where(partner == my_freq - 1, edge, left)
            right = jnp.where(partner == my_freq + 1, edge, right)
        span = slice(cells + number * TH, cells + (number + 1) * TH)
        out_ref[span, 0:columns] = block
        out_ref[span, columns : columns + TW] = right[:, columns : columns + TW]
        out_ref[span, LANES - TW : LANES] = left[:, LANES - TW :]


def energies(cells, shard, weights, conduct, baseline, shards):
    rows = cells + 3 * TH
    width = -(-max(shard, baseline.shape[1] + 2 * TW) // LANES) * LANES
    return pl.pallas_call(
        functools.partial(energy_kernel, cells, shard, len(shards)),
        in_specs=[pl.BlockSpec(memory_space=pltpu.VMEM)] * (3 + len(shards)),
        out_specs=pl.BlockSpec(memory_space=pltpu.VMEM),
        out_shape=jax.ShapeDtypeStruct((rows, width), jnp.float32),
        compiler_params=pltpu.CompilerParams(vmem_limit_bytes=VMEM_LIMIT),
        name="energies",
    )(weights, conduct, baseline, *shards)


def diffuse_kernel(cells, shard, strips_ref, out_ref, field_ref):
    pos_count, _, width = strips_ref.shape
    tile_rows = pos_count
    tile_cols = shard // tile_rows
    groups = pos_count // TH
    my_pos = lax.axis_index("pos")
    tile_row = lax.broadcasted_iota(jnp.int32, (tile_rows, width), 0)
    spot = lax.broadcasted_iota(jnp.int32, (tile_rows, width), 1)
    here = (spot % tile_rows == tile_row) & (spot < shard)
    source = lax.broadcasted_iota(jnp.int32, (width, LANES), 0)
    target = lax.broadcasted_iota(jnp.int32, (width, LANES), 1)
    field = jnp.zeros((TH * tile_rows, LANES), jnp.float32)
    for group in range(groups):
        left = 1 if group * 2 >= groups else 0
        for cell in range(cells):
            col = (source // tile_rows - left) * TW + group * cells + cell
            place = ((target == (col + LANES) % LANES) & (source < shard)).astype(jnp.float32)
            spread = []
            for row in range(TH):
                line = strips_ref[row * groups + group, pl.ds(cell, 1), :]
                spread.append(jnp.where(here, jnp.broadcast_to(line, (tile_rows, width)), 0.0))
            field = field + jnp.dot(
                jnp.concatenate(spread, axis=0), place, precision=HIGHEST, preferred_element_type=jnp.float32
            )

    def strip(which, row):
        return strips_ref[:, cells + which * TH + row, 0:LANES]

    across_k = [strip(0, row) for row in range(TH)]
    along_k = [strip(1, row) for row in range(TH)]
    field = [field[row * tile_rows : (row + 1) * tile_rows] + strip(2, row) for row in range(TH)]

    def above(rows, row):
        if row:
            return rows[row - 1]
        return jnp.where(tile_row[:, :LANES] == 0, 0.0, pltpu.roll(rows[TH - 1], 1, 0))

    def below(rows, row):
        if row < TH - 1:
            return rows[row + 1]
        return jnp.where(tile_row[:, :LANES] == tile_rows - 1, 0.0, pltpu.roll(rows[0], tile_rows - 1, 0))

    north_k = [jnp.minimum(across_k[r], above(across_k, r)) for r in range(TH)]
    south_k = [jnp.minimum(across_k[r], below(across_k, r)) for r in range(TH)]
    west_k = [jnp.minimum(k, pltpu.roll(k, 1, 1)) for k in along_k]
    east_k = [jnp.minimum(k, pltpu.roll(k, LANES - 1, 1)) for k in along_k]
    for _ in range(PASSES):
        field = [
            field[r]
            + north_k[r] * (above(field, r) - field[r])
            + south_k[r] * (below(field, r) - field[r])
            + west_k[r] * (pltpu.roll(field[r], 1, 1) - field[r])
            + east_k[r] * (pltpu.roll(field[r], LANES - 1, 1) - field[r])
            for r in range(TH)
        ]
    for row in range(TH):
        field_ref[...] = field[row]
        out_ref[pl.ds(row, 1), :] = field_ref[pl.ds(my_pos, 1), 0 : out_ref.shape[1]]


def diffuse(cells, shard, strips, columns):
    return pl.pallas_call(
        functools.partial(diffuse_kernel, cells, shard),
        in_specs=[pl.BlockSpec(memory_space=pltpu.VMEM)],
        out_specs=pl.BlockSpec(memory_space=pltpu.VMEM),
        out_shape=jax.ShapeDtypeStruct((TH, columns), jnp.float32),
        scratch_shapes=[pltpu.VMEM((strips.shape[0], LANES), jnp.float32)],
        compiler_params=pltpu.CompilerParams(vmem_limit_bytes=VMEM_LIMIT),
        name="diffuse",
    )(strips)


def swap(array, axis, distance):
    return lax.ppermute(array, axis, [(i, i ^ distance) for i in range(lax.axis_size(axis))])


def body(footprint, basis, weights, conduct, baseline):
    pos_local, freq_local, doubled, rank = basis.shape
    elements = doubled // 2
    foot = footprint.shape[1]
    pos_count = lax.axis_size("pos")
    freq_count = lax.axis_size("freq")
    columns = baseline.shape[1]
    sizes = (
        pos_count,
        freq_local * freq_count,
        pos_local * pos_count,
        elements,
        pos_local,
        freq_local,
        foot,
    )
    ids = footprint.reshape(pos_count, pos_local * foot)
    split = basis.reshape(pos_local, freq_local, 2, elements, rank)
    groups = pos_count // TH
    half = groups // 2
    parts = [None] * pos_count
    rounds = (
        tuple(range(3 * groups, 4 * groups)),
        tuple(range(2 * groups, 2 * groups + half)) + tuple(range(groups, groups + half)),
        tuple(range(2 * groups + half, 3 * groups)) + tuple(range(groups + half, 2 * groups)),
        tuple(range(groups)),
    )
    operands, after = (footprint, split), ()
    for turn, distances in enumerate(rounds):
        sent = project(sizes, rounds, turn, operands, after)
        for number, distance in enumerate(distances):
            parts[distance] = swap(sent[number], "pos", distance) if distance else sent[number]
        if turn == 0:
            operands = tuple(sent[groups:])
        after = (sent[0],)
        if turn == 2:
            after += tuple(parts[-groups:])
    cells, shard = CELLS // pos_count, (TILE_DEV // freq_count + 1) * pos_count
    tiles = gather_tiles(freq_count, ids, conduct, baseline, parts)
    shards = [swap(tiles[d], "freq", d) if d else tiles[d] for d in range(freq_count)]
    strip = energies(cells, shard, weights.reshape(1, rank), conduct, baseline, shards)
    strips = lax.all_gather(strip, "pos")
    return diffuse(cells, shard, strips, columns)


def solution(mesh):
    return jax.shard_map(
        body,
        mesh=mesh,
        in_specs=(P(), P("pos", "freq", None, None), P(), P(None, "pos", "freq"), P("pos", "freq")),
        out_specs=P("pos", "freq"),
        check_vma=False,
    )
```

```python
import functools
import math

import jax
import jax.numpy as jnp
from jax import lax
from jax.experimental import pallas as pl
from jax.experimental.pallas import tpu as pltpu
from jax.sharding import PartitionSpec as P

TH = 4
TW = 8
CELLS = TH * TW
TILE_DEV = 32
PASSES = 3
LANES = 128
RIM_ROWS = 8
ELEM_BLOCK = 256
AHEAD = 3

elem_pitch = 0.125
cell_spacing = 0.7
top_depth = 4.0
eps_value = 1e-06

SIN_PI = tuple(
    math.sqrt(2.0) * (1.0 - 2e-6) * term
    for term in (3.1415903568267822, -5.1674065589904785, 2.5440104007720947, -0.5594624280929565)
)

HIGHEST = lax.Precision.HIGHEST
VMEM_LIMIT = 24 * 1024 * 1024
VMEM_LIMIT_FIRST = 42 * 1024 * 1024


def half_turn(turns):
    x = turns - jnp.round(turns)
    square = x * x
    s = SIN_PI[-1]
    for term in SIN_PI[-2::-1]:
        s = s * square + term
    s = s * x
    rest = 2.0 - s * s
    return rest * lax.rsqrt(rest), s, rest - 1.0


def waves(distance, first_turns, step_turns, count):
    c, s, cosine = half_turn(first_turns * distance)
    amplitude = lax.rsqrt(distance)
    last = amplitude * cosine, (amplitude * c) * s
    c, s, cosine = half_turn(step_turns * distance)
    sine = c * s
    now = last[0] * cosine - last[1] * sine, last[1] * cosine + last[0] * sine
    found = [last, now]
    twice = cosine + cosine
    for _ in range(count - 2):
        now, last = tuple(twice * a - b for a, b in zip(now, last)), now
        found.append(now)
    return found[:count]


def project_kernel(sizes, rounds, turn, waits, *refs):
    first = turn == 0
    pos_count, freqs, positions, elements, pos_local, freq_local, foot = sizes
    groups = pos_count // TH
    per_dest = TW // groups
    blocks = elements // ELEM_BLOCK
    steps = pos_local * blocks
    if first:
        (foot_ref, basis_ref), refs = refs[:2], refs[2:]
        out_refs, refs = refs[:groups], refs[groups:]
        held_ref, depth_ref, lateral_ref, element_ref, green_even, green_odd, total_ref, sems = refs
    else:
        held_ref, depth_ref, lateral_ref, element_ref = refs[:4]
        out_refs, refs = refs[4 + waits : 4 + waits + groups], refs[4 + waits + groups :]
        green_even, green_odd, total_ref = refs
    my_pos, my_freq = lax.axis_index("pos"), lax.axis_index("freq")

    def fetch(step):
        offset, block = step // blocks, step % blocks
        spot = pl.ds(block * ELEM_BLOCK, ELEM_BLOCK)
        return pltpu.make_async_copy(basis_ref.at[offset, :, :, spot, :], held_ref.at[step], sems.at[step])

    if first:
        for step in range(AHEAD):
            fetch(step).start()

    first_freq = (my_freq * freq_local).astype(jnp.float32)
    first_turns = top_depth * (0.5 + first_freq / freqs)
    step_turns = top_depth / freqs

    if first:
        scale = 1.0 / top_depth
        row = lax.broadcasted_iota(jnp.int32, (TW, LANES), 0)
        lane = lax.broadcasted_iota(jnp.int32, (TW, LANES), 1)
        places = []
        for distances in rounds:
            target = my_pos ^ functools.reduce(
                lambda rest, here: jnp.where(row // per_dest == here, distances[here], rest), range(1, groups), distances[0]
            )
            places.append((target // groups, (target % groups) * per_dest + row % per_dest))
        for offset in range(pos_local):
            pos_global = my_pos * pos_local + offset
            centre = pos_global.astype(jnp.float32) * (cell_spacing * TW * TILE_DEV / positions)
            for piece in range(elements // LANES):
                index = (piece * LANES + lane).astype(jnp.float32)
                element_ref[offset, piece] = scale * ((index - 0.5 * (elements - 1)) * elem_pitch + centre)

            def place(entry, _, offset=offset, pos_global=pos_global):
                tile = foot_ref[pos_global, entry]
                for number, (cell_row, cell_col) in enumerate(places):
                    grid_row = ((tile // TILE_DEV) * TH + cell_row).astype(jnp.float32)
                    grid_col = ((tile % TILE_DEV) * TW + cell_col).astype(jnp.float32)
                    depth = scale * (top_depth + cell_spacing * grid_row)
                    depth_ref[number, offset, entry] = depth * depth
                    lateral_ref[number, offset, entry] = scale * (cell_spacing * grid_col)
                return 0

            lax.fori_loop(0, foot, place, 0, unroll=4)
    total_ref[...] = jnp.zeros_like(total_ref)

    def green(step, green_ref):
        offset, block = step // blocks, step % blocks
        for pair in range(foot // 2):
            entry = 2 * pair
            depth_square = depth_ref[turn, offset, pl.ds(entry, 2)].reshape(2 * TW, LANES)
            lateral = lateral_ref[turn, offset, pl.ds(entry, 2)].reshape(2 * TW, LANES)
            spot = pl.ds(entry * TW, 2 * TW)
            for sub in range(ELEM_BLOCK // LANES):
                element = element_ref[offset, block * (ELEM_BLOCK // LANES) + sub]
                across = lateral - jnp.concatenate([element, element], axis=0)
                square = depth_square + across * across
                distance = square * lax.rsqrt(square)
                for number, both in enumerate(waves(distance, first_turns, step_turns, freq_local)):
                    for part_of, wave in enumerate(both):
                        start = (number * 2 + part_of) * ELEM_BLOCK + sub * LANES
                        green_ref[spot, start : start + LANES] = wave.astype(jnp.bfloat16)

    def apply(step, green_ref):
        offset = step // blocks
        weights = held_ref[step].reshape(freq_local * 2 * ELEM_BLOCK, -1)
        gain = jnp.dot(green_ref[...], weights, preferred_element_type=jnp.float32)
        for half in range(gain.shape[1] // LANES):
            total_ref[offset, half] = total_ref[offset, half] + gain[:, half * LANES : (half + 1) * LANES]

    def run(make, into, use, out_of):
        if use is not None:
            if first:
                fetch(use).wait()
                if isinstance(use, int):
                    if use + AHEAD < steps:
                        fetch(use + AHEAD).start()
                else:
                    pl.when(use + AHEAD < steps)(lambda: fetch(use + AHEAD).start())
            apply(use, out_of)
        if make is not None:
            green(make, into)

    run(0, green_even, None, None)

    def two(pair, _):
        run(2 * pair + 1, green_odd, 2 * pair, green_even)
        run(2 * pair + 2, green_even, 2 * pair + 1, green_odd)
        return 0

    lax.fori_loop(0, steps // 2 - 1, two, 0)
    run(steps - 1, green_odd, steps - 2, green_even)
    run(None, None, steps - 1, green_odd)

    for offset in range(pos_local):
        for group in range(groups):
            for cell in range(per_dest):
                for half in range(total_ref.shape[1]):
                    out_refs[group][cell, offset * foot : (offset + 1) * foot, half * LANES : (half + 1) * LANES] = (
                        total_ref[offset, half, pl.ds(group * per_dest + cell, foot, stride=TW), :]
                    )


def project(sizes, rounds, turn, operands, after):
    first = turn == 0
    pos_count, freqs, positions, elements, pos_local, freq_local, foot = sizes
    groups = pos_count // TH
    per_dest = TW // groups
    basis = operands[1] if first else operands[0]
    rank = basis.shape[-1]
    rows = foot * TW
    steps = pos_local * elements // ELEM_BLOCK
    flops = 2 * pos_local * rows * freq_local * 2 * elements * rank

    def shape(*dims, dtype=jnp.float32):
        return jax.ShapeDtypeStruct(dims, dtype)

    vmem, smem = pl.BlockSpec(memory_space=pltpu.VMEM), pl.BlockSpec(memory_space=pltpu.SMEM)
    out_shape = [shape(per_dest, pos_local * foot, rank)] * groups
    if first:
        in_specs = [smem, pl.BlockSpec(memory_space=pl.ANY)]
        out_shape += [
            shape(steps, freq_local, 2, ELEM_BLOCK, rank, dtype=jnp.bfloat16),
            shape(len(rounds), pos_local, foot, TW, LANES),
            shape(len(rounds), pos_local, foot, TW, LANES),
            shape(pos_local, elements // LANES, TW, LANES),
        ]
    else:
        in_specs = [vmem] * 4 + [pl.BlockSpec(memory_space=pl.ANY)] * len(after)
    green = pltpu.VMEM((rows, freq_local * 2 * ELEM_BLOCK), jnp.bfloat16)
    return pl.pallas_call(
        functools.partial(project_kernel, sizes, rounds, turn, len(after)),
        in_specs=in_specs,
        out_specs=[vmem] * len(out_shape),
        out_shape=out_shape,
        scratch_shapes=[green, green, pltpu.VMEM((pos_local, rank // LANES, rows, LANES), jnp.float32)]
        + ([pltpu.SemaphoreType.DMA((steps,))] if first else []),
        compiler_params=pltpu.CompilerParams(vmem_limit_bytes=VMEM_LIMIT_FIRST if first else VMEM_LIMIT),
        cost_estimate=pl.CostEstimate(flops=flops, bytes_accessed=flops, transcendentals=0),
        name=f"project_{turn}",
    )(*operands, *after)


def two_terms(values):
    high = values.astype(jnp.bfloat16)
    return high, (values - high.astype(jnp.float32)).astype(jnp.bfloat16)


def rim_spot(last, number):
    start = last + number % 2 * TH
    return slice(start, start + TH), number // 2 * LANES


def gather_kernel(pos_count, freq_count, tile_rows, shard, ids_ref, conduct_ref, baseline_ref, *refs):
    in_refs, out_refs = refs[:pos_count], refs[pos_count:]
    cells, entries, rank = in_refs[0].shape
    columns = baseline_ref.shape[1]
    tile_cols = shard // tile_rows
    groups = pos_count // TH
    my_pos, my_freq = lax.axis_index("pos"), lax.axis_index("freq")
    left = (lax.rem(my_pos, groups) * 2 >= groups).astype(jnp.int32)
    row = lax.broadcasted_iota(jnp.int32, (shard, entries), 0)
    wanted = (row % tile_rows) * TILE_DEV + row // tile_rows - left
    hot = []
    for other in range(freq_count):
        base = (my_freq ^ other) * (tile_cols - 1)
        col = row // tile_rows - left + base
        hot_row = []
        for source in range(pos_count):
            ids = ids_ref[pl.ds(my_pos ^ source, 1), :]
            hit = (wanted + base == ids) & (col >= 0) & (col < TILE_DEV)
            hot_row.append(hit.astype(jnp.float32).astype(jnp.bfloat16))
        hot_row = jnp.concatenate(hot_row, axis=1)
        hot.append(jnp.concatenate([hot_row] * 2, axis=1))
    for cell in range(cells):
        values = jnp.concatenate([ref[cell] for ref in in_refs], axis=0)
        terms = jnp.concatenate(two_terms(values), axis=0)
        for other in range(freq_count):
            span = slice(cell * shard, (cell + 1) * shard)
            out_refs[other][span, :] = jnp.dot(hot[other], terms, preferred_element_type=jnp.float32)
    last = cells * shard
    for ref in out_refs[1:]:
        for number, block in enumerate((conduct_ref[0], conduct_ref[1], baseline_ref[...])):
            rows, lane = rim_spot(last, number)
            ref[rows, lane + columns : lane + columns + TW] = block[:, :TW]
            ref[rows, lane + LANES - TW : lane + LANES] = block[:, columns - TW :]


def gather_tiles(freq_count, ids, conduct, baseline, parts):
    pos_count = len(parts)
    cells, entries, rank = parts[0].shape
    tile_rows = pos_count
    shard = (TILE_DEV // freq_count + 1) * tile_rows
    return pl.pallas_call(
        functools.partial(gather_kernel, pos_count, freq_count, tile_rows, shard),
        in_specs=[pl.BlockSpec(memory_space=pltpu.VMEM)] * (3 + pos_count),
        out_specs=[pl.BlockSpec(memory_space=pltpu.VMEM)] * freq_count,
        out_shape=[jax.ShapeDtypeStruct((cells * shard, rank), jnp.float32)]
        + [jax.ShapeDtypeStruct((cells * shard + RIM_ROWS, rank), jnp.float32)] * (freq_count - 1),
        compiler_params=pltpu.CompilerParams(vmem_limit_bytes=VMEM_LIMIT),
        name="tiles",
    )(ids, conduct, baseline, *parts)


def energy_kernel(cells, shard, freq_count, weights_ref, conduct_ref, baseline_ref, *refs):
    in_refs, out_ref = refs[:freq_count], refs[freq_count]
    rank = in_refs[0].shape[1]
    my_freq = lax.axis_index("freq")
    weights = jnp.broadcast_to(weights_ref[...], (8, rank))
    for cell in range(cells):
        span = slice(cell * shard, (cell + 1) * shard)
        summed = in_refs[0][span, :]
        for ref in in_refs[1:]:
            summed = summed + ref[span, :]
        energy = lax.dot_general(
            weights,
            summed * summed,
            (((1,), (1,)), ((), ())),
            precision=HIGHEST,
            preferred_element_type=jnp.float32,
        )
        out_ref[cell : cell + 1, 0:shard] = jnp.sqrt(energy[0:1] / rank + eps_value)
    last = cells * shard
    columns = baseline_ref.shape[1]
    for number, block in enumerate((conduct_ref[0], conduct_ref[1], baseline_ref[...])):
        rows, lane = rim_spot(last, number)
        left = jnp.zeros((TH, LANES), jnp.float32)
        right = jnp.zeros((TH, LANES), jnp.float32)
        for distance in range(1, freq_count):
            edge = in_refs[distance][rows, lane : lane + LANES]
            partner = my_freq ^ distance
            left = jnp.where(partner == my_freq - 1, edge, left)
            right = jnp.where(partner == my_freq + 1, edge, right)
        span = slice(cells + number * TH, cells + (number + 1) * TH)
        out_ref[span, 0:columns] = block
        out_ref[span, columns : columns + TW] = right[:, columns : columns + TW]
        out_ref[span, LANES - TW : LANES] = left[:, LANES - TW :]


def energies(cells, shard, weights, conduct, baseline, shards):
    rows = cells + 3 * TH
    width = -(-max(shard, baseline.shape[1] + 2 * TW) // LANES) * LANES
    return pl.pallas_call(
        functools.partial(energy_kernel, cells, shard, len(shards)),
        in_specs=[pl.BlockSpec(memory_space=pltpu.VMEM)] * (3 + len(shards)),
        out_specs=pl.BlockSpec(memory_space=pltpu.VMEM),
        out_shape=jax.ShapeDtypeStruct((rows, width), jnp.float32),
        compiler_params=pltpu.CompilerParams(vmem_limit_bytes=VMEM_LIMIT),
        name="energies",
    )(weights, conduct, baseline, *shards)


def diffuse_kernel(cells, shard, strips_ref, out_ref, field_ref):
    pos_count, _, width = strips_ref.shape
    tile_rows = pos_count
    tile_cols = shard // tile_rows
    groups = pos_count // TH
    my_pos = lax.axis_index("pos")
    tile_row = lax.broadcasted_iota(jnp.int32, (tile_rows, width), 0)
    spot = lax.broadcasted_iota(jnp.int32, (tile_rows, width), 1)
    here = (spot % tile_rows == tile_row) & (spot < shard)
    source = lax.broadcasted_iota(jnp.int32, (width, LANES), 0)
    target = lax.broadcasted_iota(jnp.int32, (width, LANES), 1)
    field = jnp.zeros((TH * tile_rows, LANES), jnp.float32)
    for group in range(groups):
        left = 1 if group * 2 >= groups else 0
        for cell in range(cells):
            col = (source // tile_rows - left) * TW + group * cells + cell
            place = ((target == (col + LANES) % LANES) & (source < shard)).astype(jnp.float32)
            spread = []
            for row in range(TH):
                line = strips_ref[row * groups + group, pl.ds(cell, 1), :]
                spread.append(jnp.where(here, jnp.broadcast_to(line, (tile_rows, width)), 0.0))
            field = field + jnp.dot(
                jnp.concatenate(spread, axis=0), place, precision=HIGHEST, preferred_element_type=jnp.float32
            )

    def strip(which, row):
        return strips_ref[:, cells + which * TH + row, 0:LANES]

    across_k = [strip(0, row) for row in range(TH)]
    along_k = [strip(1, row) for row in range(TH)]
    field = [field[row * tile_rows : (row + 1) * tile_rows] + strip(2, row) for row in range(TH)]

    def above(rows, row):
        if row:
            return rows[row - 1]
        return jnp.where(tile_row[:, :LANES] == 0, 0.0, pltpu.roll(rows[TH - 1], 1, 0))

    def below(rows, row):
        if row < TH - 1:
            return rows[row + 1]
        return jnp.where(tile_row[:, :LANES] == tile_rows - 1, 0.0, pltpu.roll(rows[0], tile_rows - 1, 0))

    north_k = [jnp.minimum(across_k[r], above(across_k, r)) for r in range(TH)]
    south_k = [jnp.minimum(across_k[r], below(across_k, r)) for r in range(TH)]
    west_k = [jnp.minimum(k, pltpu.roll(k, 1, 1)) for k in along_k]
    east_k = [jnp.minimum(k, pltpu.roll(k, LANES - 1, 1)) for k in along_k]
    for _ in range(PASSES):
        field = [
            field[r]
            + north_k[r] * (above(field, r) - field[r])
            + south_k[r] * (below(field, r) - field[r])
            + west_k[r] * (pltpu.roll(field[r], 1, 1) - field[r])
            + east_k[r] * (pltpu.roll(field[r], LANES - 1, 1) - field[r])
            for r in range(TH)
        ]
    for row in range(TH):
        field_ref[...] = field[row]
        out_ref[pl.ds(row, 1), :] = field_ref[pl.ds(my_pos, 1), 0 : out_ref.shape[1]]


def diffuse(cells, shard, strips, columns):
    return pl.pallas_call(
        functools.partial(diffuse_kernel, cells, shard),
        in_specs=[pl.BlockSpec(memory_space=pltpu.VMEM)],
        out_specs=pl.BlockSpec(memory_space=pltpu.VMEM),
        out_shape=jax.ShapeDtypeStruct((TH, columns), jnp.float32),
        scratch_shapes=[pltpu.VMEM((strips.shape[0], LANES), jnp.float32)],
        compiler_params=pltpu.CompilerParams(vmem_limit_bytes=VMEM_LIMIT),
        name="diffuse",
    )(strips)


def swap(array, axis, distance):
    return lax.ppermute(array, axis, [(i, i ^ distance) for i in range(lax.axis_size(axis))])


def body(footprint, basis, weights, conduct, baseline):
    pos_local, freq_local, doubled, rank = basis.shape
    elements = doubled // 2
    foot = footprint.shape[1]
    pos_count = lax.axis_size("pos")
    freq_count = lax.axis_size("freq")
    columns = baseline.shape[1]
    sizes = (
        pos_count,
        freq_local * freq_count,
        pos_local * pos_count,
        elements,
        pos_local,
        freq_local,
        foot,
    )
    ids = footprint.reshape(pos_count, pos_local * foot)
    split = basis.reshape(pos_local, freq_local, 2, elements, rank)
    groups = pos_count // TH
    parts = [None] * pos_count
    rounds = (
        tuple(range(3 * groups, 4 * groups)),
        tuple(range(2 * groups, 3 * groups)),
        tuple(range(groups, 2 * groups)),
        tuple(range(groups)),
    )
    operands, after = (footprint, split), ()
    for turn, distances in enumerate(rounds):
        sent = project(sizes, rounds, turn, operands, after)
        for number, distance in enumerate(distances):
            parts[distance] = swap(sent[number], "pos", distance) if distance else sent[number]
        if turn == 0:
            operands = tuple(sent[groups:])
        after = (sent[0],)
        if turn == 2:
            after += tuple(parts[-groups:])
    cells, shard = CELLS // pos_count, (TILE_DEV // freq_count + 1) * pos_count
    tiles = gather_tiles(freq_count, ids, conduct, baseline, parts)
    shards = [swap(tiles[d], "freq", d) if d else tiles[d] for d in range(freq_count)]
    strip = energies(cells, shard, weights.reshape(1, rank), conduct, baseline, shards)
    strips = lax.all_gather(strip, "pos")
    return diffuse(cells, shard, strips, columns)


def solution(mesh):
    return jax.shard_map(
        body,
        mesh=mesh,
        in_specs=(P(), P("pos", "freq", None, None), P(), P(None, "pos", "freq"), P("pos", "freq")),
        out_specs=P("pos", "freq"),
        check_vma=False,
    )
```
